32 devices in a mesh: event: 4 (over y, core), gx: 2 (over x), gy: 4 (over z).
Axes of the slice: x: 2, y: 2, z: 4, core: 2. Of those that a mesh axis runs over, the one named last changes fastest.
Arguments:
- adjoint_now: float32 [4, 3, 32, 32, 128], P('event', None, 'gx', 'gy'), may hold values from -6 to 6
- adjoint_old: float32 [4, 3, 32, 32, 128], P('event', None, 'gx', 'gy'), may hold values from -6 to 6
- bulk_memory: float32 [4, 3, 32, 32, 128], P('event', None, 'gx', 'gy'), may hold values from -4 to 4
- shear_memory: float32 [4, 3, 3, 32, 32, 128], P('event', None, None, 'gx', 'gy'), may hold values from -4 to 4
- forward_strain: float32 [4, 2, 4, 32, 32, 128], P('event', None, None, 'gx', 'gy'), may hold values from -6 to 6
- bulk_modulus: float32 [32, 32, 128], P('gx', 'gy'), may hold values from 0.5 to 1.5
- shear_modulus: float32 [32, 32, 128], P('gx', 'gy'), may hold values from 0.2 to 0.8
- buoyancy: float32 [32, 32, 128], P('gx', 'gy'), may hold values from 0.5 to 2
- bulk_atten: float32 [32, 32, 128], P('gx', 'gy'), may hold values from 0.05 to 0.5
- shear_atten: float32 [32, 32, 128], P('gx', 'gy'), may hold values from 0.05 to 0.5
- relax_time: float32 [3], replicated, may hold values from 0.3 to 30
- mechanism_weight: float32 [3], replicated, may hold values from 0.5 to 2
- event_slowness: float32 [4, 3], P('event'), may hold values from -1.5 to 1.5
- event_amplitude: float32 [4, 3], P('event'), may hold values from -4 to 4
- event_onset: float32 [4], P('event'), may hold values from -1.5 to 1.5
- boundary_cells: int32 [2, 4, 1024], P('gx', 'gy'), may hold values from 0 to 16383, as said below
- boundary_count: int32 [2, 4], P('gx', 'gy'), may hold values from 1 to 1024, as said below
Outputs:
- adjoint_next: float32 [4, 3, 32, 32, 128], P('event', None, 'gx', 'gy')
- adjoint_before: float32 [4, 3, 32, 32, 128], P('event', None, 'gx', 'gy')
- bulk_next: float32 [4, 3, 32, 32, 128], P('event', None, 'gx', 'gy')
- shear_next: float32 [4, 3, 3, 32, 32, 128], P('event', None, None, 'gx', 'gy')
- grad_bulk: float32 [32, 32, 128], P('gx', 'gy')
- grad_shear: float32 [32, 32, 128], P('gx', 'gy')
The draws below stay inside these ranges and needn't reach their ends.
Inputs may be any that keep to these rules, and one draw needn't show every extreme that they name: `boundary_cells`: within one device the 1024 cell numbers are distinct. `boundary_count`: devices on the lateral edge of the grid hold 512 to 1024 live cells, and one of them exactly 1024; the others at most 256.
All inputs are finite; a program needn't handle non-finite values.
Results may differ from the reference program's by a relative error of at most 0.0001.
Values sent between devices are 32-bit elements; how exact they have to be, the bound alone decides.
No kernel may reach another device: no remote copies, remote signals or barrier semaphores. Data moves between devices by JAX's collectives and lax.ppermute only.
A program may use at most 64 MiB of HBM per device.

```python
import math
import jax
import jax.numpy as jnp

CX = 16
CY = 8
NZ = 128
MECH = 3
STEPS = 2
EVENTS = 4
NX = 32
NY = 32
CAP = 1024
N_GX = 2
N_GY = 4


def draw_boundary_cells(key, part):
    keys = jax.random.split(key, N_GX * N_GY)
    picks = jax.vmap(lambda single: jax.random.permutation(single, CX * CY * NZ)[:CAP])(keys)
    return picks.reshape(N_GX, N_GY, CAP).astype(jnp.int32)


def draw_boundary_count(key, part):
    inner_key = jax.random.fold_in(key, 11)
    edge_key = jax.random.fold_in(key, 23)
    pick_key = jax.random.fold_in(key, 37)
    inner = jax.random.randint(inner_key, (N_GX, N_GY), 1, CAP // 4 + 1)
    outer = jax.random.randint(edge_key, (N_GX, N_GY), CAP // 2, CAP + 1)
    rows = jnp.arange(N_GX)[:, None]
    columns = jnp.arange(N_GY)[None, :]
    edge = (rows == 0) | (rows == N_GX - 1) | (columns == 0) | (columns == N_GY - 1)
    chosen = jax.random.randint(pick_key, (), 0, N_GX)
    fullest = (rows == chosen) & (columns == 0)
    counts = jnp.where(edge, outer, inner)
    counts = jnp.where(fullest, CAP, counts)
    return counts.astype(jnp.int32)


def steps_of(stream_key, dims, pieces, smallest, largest):
    level, own = 1.0, jax.random.fold_in(stream_key, 6)
    for axis_at, parts in pieces:
        steps = jnp.exp(jax.random.uniform(jax.random.fold_in(own, axis_at), (parts,), jnp.float32, smallest / len(pieces), largest / len(pieces)))
        level = level * jnp.repeat(steps, dims[axis_at] // parts).reshape([-1 if axis == axis_at else 1 for axis in range(len(dims))])
    return level


def bell_draw(own_key, shape, scale, reach, pieces=(), kind=jnp.bfloat16):
    entries = jax.random.normal(own_key, shape, jnp.float32) * scale
    if len(pieces) > 0:
        entries = steps_of(own_key, shape, pieces, -0.22, 0.18) * entries
    return jnp.clip(entries, min=-reach, max=reach).astype(kind)


def setup_inputs(seed: int = 0) -> dict:
    streams_of = jax.random.split(jax.random.key(seed), 18)
    return {
        "adjoint_now": bell_draw(streams_of[0], (EVENTS, 3, NX, NY, NZ), 1.0, 6.0, ((0, 4), (2, 2), (3, 4)), jnp.float32),
        "adjoint_old": bell_draw(streams_of[1], (EVENTS, 3, NX, NY, NZ), 1.0, 6.0, ((0, 4), (2, 2), (3, 4)), jnp.float32),
        "bulk_memory": bell_draw(streams_of[2], (EVENTS, MECH, NX, NY, NZ), 0.3, 4.0, ((0, 4), (2, 2), (3, 4)), jnp.float32),
        "shear_memory": bell_draw(streams_of[3], (EVENTS, MECH, 3, NX, NY, NZ), 0.3, 4.0, ((0, 4), (3, 2), (4, 4)), jnp.float32),
        "forward_strain": bell_draw(streams_of[4], (EVENTS, STEPS, 4, NX, NY, NZ), 1.0, 6.0, ((0, 4), (3, 2), (4, 4)), jnp.float32),
        "bulk_modulus": jnp.clip(0.5 + 1.0 * jax.random.uniform(streams_of[5], (NX, NY, NZ), jnp.float32) ** steps_of(streams_of[5], (NX, NY, NZ), ((0, 2), (1, 4)), -0.2, 0.2), 0.5, 1.5),
        "shear_modulus": jnp.clip(0.2 + 0.6 * jax.random.uniform(streams_of[6], (NX, NY, NZ), jnp.float32) ** steps_of(streams_of[6], (NX, NY, NZ), ((0, 2), (1, 4)), -0.2, 0.2), 0.2, 0.8),
        "buoyancy": jnp.clip(0.5 + 1.5 * jax.random.uniform(streams_of[7], (NX, NY, NZ), jnp.float32) ** steps_of(streams_of[7], (NX, NY, NZ), ((0, 2), (1, 4)), -0.2, 0.2), 0.5, 2.0),
        "bulk_atten": jnp.clip(jnp.exp(math.log(0.5) - 2.3025851 * jax.random.uniform(streams_of[8], (NX, NY, NZ), jnp.float32) ** steps_of(streams_of[8], (NX, NY, NZ), ((0, 2), (1, 4)), -0.2, 0.2)), 0.05, 0.5),
        "shear_atten": jnp.clip(jnp.exp(math.log(0.5) - 2.3025851 * jax.random.uniform(streams_of[9], (NX, NY, NZ), jnp.float32) ** steps_of(streams_of[9], (NX, NY, NZ), ((0, 2), (1, 4)), -0.2, 0.2)), 0.05, 0.5),
        "relax_time": jnp.clip(jnp.exp(jax.random.uniform(streams_of[10], (MECH,), jnp.float32, math.log(0.3), math.log(30.0))), 0.3, 30.0),
        "mechanism_weight": jnp.clip(jnp.exp(jax.random.uniform(streams_of[11], (MECH,), jnp.float32, math.log(0.5), math.log(2.0))), 0.5, 2.0),
        "event_slowness": jnp.clip(jax.random.uniform(streams_of[12], (EVENTS, 3), jnp.float32, -1.5, 1.5) * steps_of(streams_of[12], (EVENTS, 3), ((0, 4),), -0.4, 0.0), -1.5, 1.5),
        "event_amplitude": bell_draw(streams_of[13], (EVENTS, 3), 1.0, 4.0, ((0, 4),), jnp.float32),
        "event_onset": jnp.clip(jax.random.uniform(streams_of[14], (EVENTS,), jnp.float32, -1.5, 1.5) * steps_of(streams_of[14], (EVENTS,), ((0, 4),), -0.4, 0.0), -1.5, 1.5),
        "boundary_cells": draw_boundary_cells(jax.random.fold_in(streams_of[17], 71), 0),
        "boundary_count": draw_boundary_count(jax.random.fold_in(streams_of[17], 71), 0),
    }


time_step = 0.3


def central_div(padded):
    dx = padded[0, 2:, 1:-1] - padded[0, :-2, 1:-1]
    dy = padded[1, 1:-1, 2:] - padded[1, 1:-1, :-2]
    deep = jnp.pad(padded[2, 1:-1, 1:-1], ((0, 0), (0, 0), (1, 1)))
    dz = deep[..., 2:] - deep[..., :-2]
    return 0.5 * (dx + dy + dz)


def laplace(padded):
    centre = padded[:, 1:-1, 1:-1, :]
    total = padded[:, 2:, 1:-1, :] + padded[:, :-2, 1:-1, :]
    total = total + padded[:, 1:-1, 2:, :] + padded[:, 1:-1, :-2, :]
    deep = jnp.pad(centre, ((0, 0), (0, 0), (0, 0), (1, 1)))
    total = total + deep[..., 2:] + deep[..., :-2]
    return total - 6.0 * centre


def gradient(padded):
    along_x = 0.5 * (padded[2:, 1:-1] - padded[:-2, 1:-1])
    along_y = 0.5 * (padded[1:-1, 2:] - padded[1:-1, :-2])
    deep = jnp.pad(padded[1:-1, 1:-1], ((0, 0), (0, 0), (1, 1)))
    along_z = 0.5 * (deep[..., 2:] - deep[..., :-2])
    return jnp.stack([along_x, along_y, along_z], 0)


def ricker(tau):
    return (1.0 - 2.0 * tau * tau) * jnp.exp(-tau * tau)


def reference(adjoint_now, adjoint_old, bulk_memory, shear_memory, forward_strain, bulk_modulus, shear_modulus, buoyancy, bulk_atten, shear_atten, relax_time, mechanism_weight, event_slowness, event_amplitude, event_onset, boundary_cells, boundary_count):
    decay = jnp.exp(-time_step / relax_time)
    gain = (1.0 - decay) * mechanism_weight
    flat = boundary_cells
    local_x = flat // (CY * NZ)
    local_y = (flat // NZ) % CY
    local_z = flat % NZ
    block_x = jnp.arange(N_GX, dtype=jnp.int32)[:, None, None] * CX
    block_y = jnp.arange(N_GY, dtype=jnp.int32)[None, :, None] * CY
    whole_x = block_x + local_x
    whole_y = block_y + local_y
    slots = jnp.arange(CAP, dtype=jnp.int32)[None, None, :]
    live = (slots < boundary_count[:, :, None]).astype(jnp.float32)
    pos_x = whole_x.astype(jnp.float32) / NX
    pos_y = whole_y.astype(jnp.float32) / NY
    pos_z = local_z.astype(jnp.float32) / NZ
    target = (whole_x * (NY * NZ) + whole_y * NZ + local_z).reshape(-1)
    out_now, out_old, out_bulk, out_shear = [], [], [], []
    grad_bulk = jnp.zeros((NX, NY, NZ), jnp.float32)
    grad_shear = jnp.zeros((NX, NY, NZ), jnp.float32)
    for event in range(EVENTS):
        wave = adjoint_now[event]
        older = adjoint_old[event]
        zeta = bulk_memory[event]
        memo = shear_memory[event]
        slow = event_slowness[event]
        delay = slow[0] * pos_x + slow[1] * pos_y + slow[2] * pos_z
        for step in range(STEPS):
            tau = step * time_step - event_onset[event] - delay
            pulse = (ricker(tau) * live).reshape(-1)
            drive = jnp.zeros((3, NX * NY * NZ), jnp.float32)
            drive = drive.at[:, target].add(event_amplitude[event][:, None] * pulse[None, :]).reshape(3, NX, NY, NZ)
            padded = jnp.pad(wave, ((0, 0), (1, 1), (1, 1), (0, 0)))
            diver = central_div(padded)
            lapl = laplace(padded)
            pressure = bulk_modulus * diver - jnp.sum(zeta, 0)
            push = gradient(jnp.pad(pressure, ((1, 1), (1, 1), (0, 0))))
            force = push + shear_modulus * lapl - jnp.sum(memo, 0) + drive
            fresh = 2.0 * wave - older + time_step * time_step * buoyancy * force
            zeta = decay[:, None, None, None] * zeta + gain[:, None, None, None] * (bulk_atten * bulk_modulus * diver)[None]
            memo = decay[:, None, None, None, None] * memo + gain[:, None, None, None, None] * (shear_atten * shear_modulus * lapl)[None]
            grad_bulk = grad_bulk + bulk_modulus * diver * forward_strain[event, step, 0]
            grad_shear = grad_shear + shear_modulus * jnp.sum(lapl * forward_strain[event, step, 1:], 0)
            older = wave
            wave = fresh
        out_now.append(wave)
        out_old.append(older)
        out_bulk.append(zeta)
        out_shear.append(memo)
    return (jnp.stack(out_now, 0), jnp.stack(out_old, 0), jnp.stack(out_bulk, 0), jnp.stack(out_shear, 0), grad_bulk, grad_shear)
```

```python
import functools

import jax
import jax.numpy as jnp
from jax import lax
from jax.experimental import pallas as pl
from jax.experimental.pallas import tpu as pltpu
from jax.sharding import PartitionSpec as P

TIME_STEP = 0.3
DT2 = TIME_STEP * TIME_STEP
TILE = (8, 128)

X_LIST = (
    [("wx", d) for d in (1, 2, 3, 4)]
    + [("wy", d) for d in (1, 2, 3)]
    + [("wz", d) for d in (1, 2, 3)]
    + [("kappa", d) for d in (1, 2, 3)]
    + [("zsum", d) for d in (1, 2, 3)]
    + [(f"base{c}", d) for c in range(3) for d in (1, 2)]
    + [("bb", d) for d in (1, 2)]
    + [("bbmu", d) for d in (1, 2)]
    + [("z1", 1), ("atten", 1)]
)
X_AT = {key: at for at, key in enumerate(X_LIST)}
D_LIST = [(t, 1) for t in range(4)] + [(t, 2) for t in range(3)] + [(0, 3)]


def roll(tile, shift, axis):
    return pltpu.roll(tile, shift % TILE[axis], axis)


def row_of():
    return lax.broadcasted_iota(jnp.int32, TILE, 0)


def lane_of():
    return lax.broadcasted_iota(jnp.int32, TILE, 1)


def zplus(f):
    return jnp.where(lane_of() == TILE[1] - 1, 0.0, roll(f, -1, 1))


def zminus(f):
    return jnp.where(lane_of() == 0, 0.0, roll(f, 1, 1))


def yplus(block, halo):
    b, h = roll(block, -1, 0), roll(halo, -1, 0)
    last = row_of() == TILE[0] - 1
    return jnp.where(last, h, b), jnp.where(last, b, h)


def yminus(block, halo):
    b, h = roll(block, 1, 0), roll(halo, 1, 0)
    first = row_of() == 0
    return jnp.where(first, h, b), jnp.where(first, b, h)


def decay_gain(relax_ref, weight_ref):
    decay, gain = [], []
    for l in range(relax_ref.shape[0]):
        d = jnp.exp(-TIME_STEP / jnp.full(TILE, relax_ref[l], jnp.float32))
        decay.append(d)
        gain.append((1.0 - d) * weight_ref[l])
    return decay, gain


def wave_phase(slow_ref, onset_ref, counts):
    nx, ny, cx = counts
    i, j = lax.axis_index("gx"), lax.axis_index("gy")
    py = (j * TILE[0] + row_of()).astype(jnp.float32) / float(ny * TILE[0])
    pz = lane_of().astype(jnp.float32) / float(TILE[1])
    common = slow_ref[0, 1] * py + slow_ref[0, 2] * pz + onset_ref[0]

    def at(x):
        px = jnp.full(TILE, i * cx + x, jnp.int32).astype(jnp.float32) / float(nx * cx)
        return slow_ref[0, 0] * px + common

    return at


def pulse_of(tau):
    square = tau * tau
    return (1.0 - 2.0 * square) * jnp.exp(-square)


def pack_kernel(
    counts, np_, w_ref, v_ref, bm_ref, sm_ref, kappa_ref, mu_ref, buoy_ref, at_ref, relax_ref, weight_ref,
    slow_ref, amp_ref, onset_ref, cells_ref, count_ref, *outs,
):
    nx, ny, cx = counts
    y_refs = outs[:2]
    x_refs = outs[2 : 2 + np_]
    d_refs = outs[2 + np_ : 2 + 3 * np_]
    mask_ref, base_ref, zsum_ref, z1_ref = outs[2 + 3 * np_ :]
    i, j = lax.axis_index("gx"), lax.axis_index("gy")
    rows = cx * TILE[0]
    slots = cells_ref.shape[2]
    cells = cells_ref[0]
    slot = lax.broadcasted_iota(jnp.int32, (1, slots), 1)
    live = slot < count_ref[0, 0]
    row_id = jnp.where(live, cells >> 7, -1)
    lane_id = cells & (TILE[1] - 1)
    wide = lax.broadcasted_iota(jnp.int32, (rows, slots), 0)
    hot_row = jnp.where(wide == row_id, 1.0, 0.0).astype(jnp.bfloat16)
    deep = lax.broadcasted_iota(jnp.int32, (TILE[1], slots), 0)
    hot_lane = jnp.where(deep == lane_id, 1.0, 0.0).astype(jnp.bfloat16)
    mask = lax.dot_general(
        hot_row, hot_lane, (((1,), (1,)), ((), ())), preferred_element_type=jnp.float32
    )
    mask_ref[...] = mask.reshape(cx, TILE[0], TILE[1])

    decay, _ = decay_gain(relax_ref, weight_ref)
    phase = wave_phase(slow_ref, onset_ref, counts)
    row = row_of()
    keep = ((row >> 2) ^ (j & 1)) == 1
    two_three = (row == 2) | (row == 3)
    four_five = (row == 4) | (row == 5)

    def pair(first, second):
        return jnp.where(
            two_three, roll(second, 2, 0), jnp.where(four_five, roll(second, -2, 0), first)
        )

    for x in range(cx):
        w = [w_ref[0, c, x] for c in range(3)]
        kappa, mu, atten = kappa_ref[x], mu_ref[x], at_ref[x]
        bb = DT2 * buoy_ref[x]
        bbmu = bb * mu
        pulse = pulse_of(-phase(x)) * mask_ref[x]
        base = []
        for c in range(3):
            total = sm_ref[0, 0, c, x] + sm_ref[0, 1, c, x] + sm_ref[0, 2, c, x]
            value = 2.0 * w[c] - v_ref[0, c, x] + bb * (amp_ref[0, c] * pulse - total)
            base_ref[c, x] = value
            base.append(value)
        bm = [bm_ref[0, l, x] for l in range(3)]
        zsum = bm[0] + bm[1] + bm[2]
        z1 = decay[0] * bm[0] + decay[1] * bm[1] + decay[2] * bm[2]
        zsum_ref[x] = zsum
        z1_ref[x] = z1
        third = jnp.where(
            row == 2,
            roll(z1, 2, 0),
            jnp.where(
                row == 3,
                roll(atten, 3, 0),
                jnp.where(row == 4, roll(atten, -3, 0), jnp.where(row == 5, roll(z1, -2, 0), bbmu)),
            ),
        )
        tiles = [
            (w[0], w[1]),
            (w[2], kappa),
            (zsum, third),
            (pair(base[0], base[1]), pair(base[2], bb)),
        ]
        for t, (a, b) in enumerate(tiles):
            b = roll(b, 4, 0)
            y_refs[0][t, x] = jnp.where(keep, a, b)
            y_refs[1][t, x] = jnp.where(keep, b, a)

    for p in range(np_):
        for (name, d), at in X_AT.items():
            x = jnp.where(((i ^ p) & 1) == 0, cx - d, d - 1)
            if name[0] == "w":
                value = w_ref[0, "xyz".index(name[1]), x]
            elif name == "kappa":
                value = kappa_ref[x]
            elif name == "zsum":
                value = zsum_ref[x]
            elif name == "z1":
                value = z1_ref[x]
            elif name == "atten":
                value = at_ref[x]
            elif name == "bb":
                value = DT2 * buoy_ref[x]
            elif name == "bbmu":
                value = DT2 * buoy_ref[x] * mu_ref[x]
            else:
                value = base_ref[int(name[4]), x]
            x_refs[p][at] = value
        for q in range(2):
            for at, (t, d) in enumerate(D_LIST):
                x = jnp.where(((i ^ p) & 1) == 0, cx - d, d - 1)
                d_refs[2 * p + q][at] = y_refs[q][t, x]


def first_kernel(
    counts, np_, w_ref, kappa_ref, mu_ref, buoy_ref, at_ref, strain_ref, relax_ref, weight_ref, base_ref, zsum_ref,
    z1_ref, *rest,
):
    nx, ny, cx = counts
    y_refs = rest[:2]
    x_refs = rest[2 : 2 + np_]
    d_refs = rest[2 + np_ : 2 + 3 * np_]
    (term_ref, w1_ref, d0_ref, l0_ref, d1_ref, l1_ref, pb_ref, ph_ref) = rest[2 + 3 * np_ : 10 + 3 * np_]
    (side_ref, halo_ref, p0b, p0h, d0b, d0h, w1b, w1h) = rest[10 + 3 * np_ :]
    i, j = lax.axis_index("gx"), lax.axis_index("gy")
    row = row_of()

    n = len(X_LIST)
    low_there, high_there = i > 0, i < nx - 1
    even = (i & 1) == 0

    def from_sides(pick):
        if np_ == 1:
            value = pick(0)
            return value, value
        first, second = pick(0), pick(1)
        return jnp.where(even, second, first), jnp.where(even, first, second)

    for at in range(n):
        low, high = from_sides(lambda p: x_refs[p][at])
        side_ref[at] = jnp.where(low_there, low, 0.0)
        side_ref[n + at] = jnp.where(high_there, high, 0.0)

    there = jnp.where(row < 4, (j < ny - 1).astype(jnp.int32), (j > 0).astype(jnp.int32))
    mine = (row >> 2) ^ (j & 1)
    pick0, pick1 = jnp.where(mine == 0, there, 0), jnp.where(mine == 1, there, 0)
    swap0, swap1 = roll(pick0, 4, 0), roll(pick1, 4, 0)

    def unpack(t, x, r0, r1, ok):
        if ok is not None:
            r0, r1 = jnp.where(ok, r0, 0.0), jnp.where(ok, r1, 0.0)
        a = jnp.where(pick0 == 1, r0, jnp.where(pick1 == 1, r1, 0.0))
        b = roll(jnp.where(swap0 == 1, r0, jnp.where(swap1 == 1, r1, 0.0)), 4, 0)

        def second(f, near, far):
            return jnp.where(row < 4, roll(f, -near, 0), roll(f, far, 0))

        if t == 0:
            put(("wx", x), a)
            put(("wy", x), b)
        elif t == 1:
            put(("wz", x), a)
            put(("kappa", x), b)
        elif t == 2:
            put(("zsum", x), a)
            if -2 < x < cx + 1:
                put(("bbmu", x), b)
            if 0 <= x < cx:
                put(("z1", x), second(b, 2, 2))
                put(("atten", x), second(b, 3, 3))
        else:
            put(("base0", x), a)
            put(("base1", x), second(a, 2, 2))
            put(("base2", x), b)
            put(("bb", x), second(b, 2, 2))

    names = ["wx", "wy", "wz", "kappa", "zsum", "bbmu", "z1", "atten", "base0", "base1", "base2", "bb"]

    def put(key, value):
        halo_ref[names.index(key[0]), 3 + key[1]] = value

    def halo(name, x):
        return halo_ref[names.index(name), 3 + x]

    for x in range(cx):
        for t in range(4):
            unpack(t, x, y_refs[0][t, x], y_refs[1][t, x], None)
    for at, (t, d) in enumerate(D_LIST):
        low0, high0 = from_sides(lambda p: d_refs[2 * p][at])
        low1, high1 = from_sides(lambda p: d_refs[2 * p + 1][at])
        unpack(t, -d, low0, low1, low_there)
        unpack(t, cx - 1 + d, high0, high1, high_there)

    def block(name, x):
        if x < 0:
            return side_ref[X_AT[(name, -x)]]
        if x >= cx:
            return side_ref[n + X_AT[(name, x - cx + 1)]]
        if name[0] == "w":
            return w_ref[0, "xyz".index(name[1]), x]
        if name == "kappa":
            return kappa_ref[x]
        if name == "zsum":
            return zsum_ref[x]
        if name == "z1":
            return z1_ref[x]
        if name == "atten":
            return at_ref[x]
        if name == "bb":
            return DT2 * buoy_ref[x]
        if name == "bbmu":
            return DT2 * buoy_ref[x] * mu_ref[x]
        return base_ref[int(name[4]), x]

    def divergence(get_b, get_h, x, with_halo):
        yb, yh = get_b(1, x), get_h(1, x)
        up, down = yplus(yb, yh), yminus(yb, yh)
        z = get_b(2, x)
        db = 0.5 * (get_b(0, x + 1) - get_b(0, x - 1) + (up[0] - down[0]) + (zplus(z) - zminus(z)))
        if not with_halo:
            return db, None
        z = get_h(2, x)
        dh = 0.5 * (get_h(0, x + 1) - get_h(0, x - 1) + (up[1] - down[1]) + (zplus(z) - zminus(z)))
        return db, dh

    def w_b(c, x):
        return block("w" + "xyz"[c], x)

    def w_h(c, x):
        return halo("w" + "xyz"[c], x)

    for x in range(-3, cx + 3):
        inner = -3 < x < cx + 2
        db, dh = divergence(w_b, w_h, x, inner)
        p0b[3 + x] = block("kappa", x) * db - block("zsum", x)
        if -2 < x < cx + 1:
            d0b[1 + x] = db
        if inner:
            p0h[2 + x] = halo("kappa", x) * dh - halo("zsum", x)
            if 0 <= x < cx:
                d0h[x] = dh
                d0_ref[x] = db

    def lap(get_b, get_h, c, x, with_halo):
        b, h = get_b(c, x), get_h(c, x)
        up, down = yplus(b, h), yminus(b, h)
        lb = get_b(c, x + 1) + get_b(c, x - 1) + (up[0] + down[0]) + (zplus(b) + zminus(b)) - 6.0 * b
        if not with_halo:
            return lb, None
        lh = get_h(c, x + 1) + get_h(c, x - 1) + (up[1] + down[1]) + (zplus(h) + zminus(h)) - 6.0 * h
        return lb, lh

    for x in range(-2, cx + 2):
        near = -2 < x < cx + 1
        inside = 0 <= x < cx
        bb, bbmu = block("bb", x), block("bbmu", x)
        if near:
            pb, ph = p0b[3 + x], p0h[2 + x]
            up, down = yplus(pb, ph), yminus(pb, ph)
            grad_b = [0.5 * (p0b[4 + x] - p0b[2 + x]), 0.5 * (up[0] - down[0]), 0.5 * (zplus(pb) - zminus(pb))]
            grad_h = [0.5 * (p0h[3 + x] - p0h[1 + x]), 0.5 * (up[1] - down[1]), 0.5 * (zplus(ph) - zminus(ph))]
            hbb, hbbmu = halo("bb", x), halo("bbmu", x)
        else:
            grad_b = [0.5 * (p0b[4 + x] - p0b[2 + x])]
        for c in range(3 if near else 1):
            with_halo = inside or (near and c < 2)
            lb, lh = lap(w_b, w_h, c, x, with_halo)
            value = block(f"base{c}", x) + bb * grad_b[c] + bbmu * lb
            w1b[c, 2 + x] = value
            if inside:
                l0_ref[c, x] = lb
                w1_ref[0, c, x] = value
            if with_halo:
                w1h[c, 1 + x] = halo(f"base{c}", x) + hbb * grad_h[c] + hbbmu * lh

    def w1_b(c, x):
        return w1b[c, 2 + x]

    def w1_h(c, x):
        return w1h[c, 1 + x]

    _, gain = decay_gain(relax_ref, weight_ref)
    gains = gain[0] + gain[1] + gain[2]
    for x in range(-1, cx + 1):
        inside = 0 <= x < cx
        db, dh = divergence(w1_b, w1_h, x, inside)
        kappa = block("kappa", x)
        stress = kappa * db
        pb_ref[1 + x] = stress - (block("z1", x) + gains * (block("atten", x) * kappa * d0b[1 + x]))
        if not inside:
            continue
        hk = halo("kappa", x)
        ph_ref[x] = hk * dh - (halo("z1", x) + gains * (halo("atten", x) * hk * d0h[x]))
        d1_ref[x] = db
        term_ref[0, x] = kappa * d0b[1 + x] * strain_ref[0, 0, 0, x] + stress * strain_ref[0, 1, 0, x]
        total0, total1 = None, None
        for c in range(3):
            lb, _ = lap(w1_b, w1_h, c, x, False)
            l1_ref[c, x] = lb
            part0 = l0_ref[c, x] * strain_ref[0, 0, 1 + c, x]
            part1 = lb * strain_ref[0, 1, 1 + c, x]
            total0 = part0 if total0 is None else total0 + part0
            total1 = part1 if total1 is None else total1 + part1
        mu = mu_ref[x]
        term_ref[1, x] = mu * total0 + mu * total1


def last_kernel(
    counts, w_ref, bm_ref, sm_ref, kappa_ref, mu_ref, buoy_ref, bat_ref, sat_ref, relax_ref, weight_ref, slow_ref,
    amp_ref, onset_ref, mask_ref, w1_ref, d0_ref, l0_ref, d1_ref, l1_ref, pb_ref, ph_ref, w2_ref, bn_ref, sn_ref,
):
    nx, ny, cx = counts
    decay, gain = decay_gain(relax_ref, weight_ref)
    phase = wave_phase(slow_ref, onset_ref, counts)
    for x in range(cx):
        bulk = bat_ref[x] * kappa_ref[x]
        q0, q1 = bulk * d0_ref[x], bulk * d1_ref[x]
        for l in range(3):
            now = decay[l] * bm_ref[0, l, x] + gain[l] * q0
            bn_ref[0, l, x] = decay[l] * now + gain[l] * q1
        pb = pb_ref[1 + x]
        ph = ph_ref[x]
        up, down = yplus(pb, ph), yminus(pb, ph)
        grad = [
            0.5 * (pb_ref[2 + x] - pb_ref[x]),
            0.5 * (up[0] - down[0]),
            0.5 * (zplus(pb) - zminus(pb)),
        ]
        mu = mu_ref[x]
        shear = sat_ref[x] * mu
        pulse = pulse_of(TIME_STEP - phase(x)) * mask_ref[x]
        bb = DT2 * buoy_ref[x]
        for c in range(3):
            l1 = l1_ref[c, x]
            q0, q1 = shear * l0_ref[c, x], shear * l1
            total = None
            for l in range(3):
                now = decay[l] * sm_ref[0, l, c, x] + gain[l] * q0
                sn_ref[0, l, c, x] = decay[l] * now + gain[l] * q1
                total = now if total is None else total + now
            force = grad[c] + mu * l1 - total + amp_ref[0, c] * pulse
            w2_ref[0, c, x] = 2.0 * w1_ref[0, c, x] - w_ref[0, c, x] + bb * force


def matched(value, mesh_shape, along_x, along_y, p, q):
    nx, ny = mesh_shape
    pairs = []
    for a in range(nx):
        for b in range(ny):
            c, d = a, b
            if along_x:
                c = a + 1 if a % 2 == p else a - 1
            if along_y:
                d = b + 1 if b % 2 == q else b - 1
            if not (0 <= c < nx and 0 <= d < ny):
                c, d = a, b
            pairs.append((a * ny + b, c * ny + d))
    return lax.ppermute(value, ("gx", "gy"), pairs)


def event_sum(value):
    count = lax.axis_size("event")
    if count & (count - 1):
        return lax.psum(value, "event")
    step = 1
    while step < count:
        value = value + lax.ppermute(value, "event", [(e, e ^ step) for e in range(count)])
        step *= 2
    return value


def vmem():
    return pl.BlockSpec(memory_space=pltpu.VMEM)


def smem():
    return pl.BlockSpec(memory_space=pltpu.SMEM)


def body(
    adjoint_now, adjoint_old, bulk_memory, shear_memory, forward_strain, bulk_modulus, shear_modulus, buoyancy,
    bulk_atten, shear_atten, relax_time, mechanism_weight, event_slowness, event_amplitude, event_onset,
    boundary_cells, boundary_count,
):
    nx, ny = lax.axis_size("gx"), lax.axis_size("gy")
    cx = bulk_modulus.shape[0]
    counts = (nx, ny, cx)
    np_ = 1 if nx == 2 else 2
    f32 = jnp.float32

    def field(*lead):
        return jax.ShapeDtypeStruct((*lead, *TILE), f32)

    params = pltpu.CompilerParams(vmem_limit_bytes=24 * 1024 * 1024)
    packed = pl.pallas_call(
        functools.partial(pack_kernel, counts, np_),
        out_shape=[field(4, cx)] * 2
        + [field(len(X_LIST))] * np_
        + [field(len(D_LIST))] * (2 * np_)
        + [field(cx), field(3, cx), field(cx), field(cx)],
        in_specs=[vmem()] * 8 + [smem()] * 5 + [vmem(), smem()],
        out_specs=[vmem()] * (2 + 3 * np_ + 4),
        compiler_params=params,
        name="pack",
    )(
        adjoint_now, adjoint_old, bulk_memory, shear_memory, bulk_modulus, shear_modulus, buoyancy, bulk_atten,
        relax_time, mechanism_weight, event_slowness, event_amplitude, event_onset, boundary_cells, boundary_count,
    )
    shape = (nx, ny)
    ys = [matched(packed[q], shape, False, True, 0, q) for q in range(2)]
    xs = [matched(packed[2 + p], shape, True, False, p, 0) for p in range(np_)]
    ds = [
        matched(packed[2 + np_ + 2 * p + q], shape, True, True, p, q) for p in range(np_) for q in range(2)
    ]
    mask, base, zsum, z1 = packed[2 + 3 * np_ :]

    first = pl.pallas_call(
        functools.partial(first_kernel, counts, np_),
        out_shape=[
            field(2, cx), field(1, 3, cx), field(cx), field(3, cx), field(cx), field(3, cx), field(cx + 2), field(cx),
        ],
        in_specs=[vmem()] * 6 + [smem()] * 2 + [vmem()] * (3 + 2 + 3 * np_),
        out_specs=[vmem()] * 8,
        scratch_shapes=[
            pltpu.VMEM((2 * len(X_LIST), *TILE), f32),
            pltpu.VMEM((12, cx + 6, *TILE), f32),
            pltpu.VMEM((cx + 6, *TILE), f32),
            pltpu.VMEM((cx + 4, *TILE), f32),
            pltpu.VMEM((cx + 2, *TILE), f32),
            pltpu.VMEM((cx, *TILE), f32),
            pltpu.VMEM((3, cx + 4, *TILE), f32),
            pltpu.VMEM((3, cx + 2, *TILE), f32),
        ],
        compiler_params=params,
        name="first",
    )(
        adjoint_now, bulk_modulus, shear_modulus, buoyancy, bulk_atten, forward_strain, relax_time, mechanism_weight,
        base, zsum, z1, *ys, *xs, *ds,
    )
    term, w1, d0, l0, d1, l1, pb, ph = first
    total = event_sum(term)

    w2, bulk_next, shear_next = pl.pallas_call(
        functools.partial(last_kernel, counts),
        out_shape=[field(1, 3, cx), field(1, 3, cx), field(1, 3, 3, cx)],
        in_specs=[vmem()] * 8 + [smem()] * 5 + [vmem()] * 8,
        out_specs=[vmem()] * 3,
        compiler_params=params,
        cost_estimate=pl.CostEstimate(flops=3_000_000, bytes_accessed=4_000_000, transcendentals=0),
        name="last",
    )(
        adjoint_now, bulk_memory, shear_memory, bulk_modulus, shear_modulus, buoyancy, bulk_atten, shear_atten,
        relax_time, mechanism_weight, event_slowness, event_amplitude, event_onset, mask, w1, d0, l0, d1, l1, pb, ph,
    )
    return w2, w1, bulk_next, shear_next, total[0], total[1]


def solution(mesh):
    wide = P("event", None, "gx", "gy", None)
    wider = P("event", None, None, "gx", "gy", None)
    grid = P("gx", "gy", None)
    return jax.shard_map(
        body,
        mesh=mesh,
        in_specs=(
            wide, wide, wide, wider, wider, grid, grid, grid, grid, grid, P(), P(), P("event", None),
            P("event", None), P("event"), grid, P("gx", "gy"),
        ),
        out_specs=(wide, wide, wide, wider, grid, grid),
        check_vma=False,
    )
```

```python
import functools

import jax
import jax.numpy as jnp
from jax import lax
from jax.experimental import pallas as pl
from jax.experimental.pallas import tpu as pltpu
from jax.sharding import PartitionSpec as P

TIME_STEP = 0.3
DT2 = TIME_STEP * TIME_STEP
TILE = (8, 128)

X_LIST = (
    [("wx", d) for d in (1, 2, 3, 4)]
    + [("wy", d) for d in (1, 2, 3)]
    + [("wz", d) for d in (1, 2, 3)]
    + [("kappa", d) for d in (1, 2, 3)]
    + [("zsum", d) for d in (1, 2, 3)]
    + [(f"base{c}", d) for c in range(3) for d in (1, 2)]
    + [("bb", d) for d in (1, 2)]
    + [("bbmu", d) for d in (1, 2)]
    + [("z1", 1), ("atten", 1)]
)
X_AT = {key: at for at, key in enumerate(X_LIST)}
PACK_ARGS = 15
D_LIST = [(t, 1) for t in range(4)] + [(t, 2) for t in range(3)] + [(0, 3)]


def roll(tile, shift, axis):
    return pltpu.roll(tile, shift % TILE[axis], axis)


def row_of():
    return lax.broadcasted_iota(jnp.int32, TILE, 0)


def lane_of():
    return lax.broadcasted_iota(jnp.int32, TILE, 1)


def zplus(f):
    return jnp.where(lane_of() == TILE[1] - 1, 0.0, roll(f, -1, 1))


def zminus(f):
    return jnp.where(lane_of() == 0, 0.0, roll(f, 1, 1))


def yplus(block, halo):
    b, h = roll(block, -1, 0), roll(halo, -1, 0)
    last = row_of() == TILE[0] - 1
    return jnp.where(last, h, b), jnp.where(last, b, h)


def yminus(block, halo):
    b, h = roll(block, 1, 0), roll(halo, 1, 0)
    first = row_of() == 0
    return jnp.where(first, h, b), jnp.where(first, b, h)


def decay_gain(relax_ref, weight_ref):
    decay, gain = [], []
    for l in range(relax_ref.shape[0]):
        d = jnp.exp(-TIME_STEP / jnp.full(TILE, relax_ref[l], jnp.float32))
        decay.append(d)
        gain.append((1.0 - d) * weight_ref[l])
    return decay, gain


def wave_phase(slow_ref, onset_ref, counts):
    nx, ny, cx = counts
    i, j = lax.axis_index("gx"), lax.axis_index("gy")
    py = (j * TILE[0] + row_of()).astype(jnp.float32) / float(ny * TILE[0])
    pz = lane_of().astype(jnp.float32) / float(TILE[1])
    common = slow_ref[0, 1] * py + slow_ref[0, 2] * pz + onset_ref[0]

    def at(x):
        px = jnp.full(TILE, i * cx + x, jnp.int32).astype(jnp.float32) / float(nx * cx)
        return slow_ref[0, 0] * px + common

    return at


def pulse_of(tau):
    square = tau * tau
    return (1.0 - 2.0 * square) * jnp.exp(-square)


def pack_kernel(
    counts, np_, *refs,
):
    nx, ny, cx = counts
    count_ref, onset_ref, given, rest = refs[0], refs[1], refs[2:PACK_ARGS], refs[PACK_ARGS:]
    outs, held, sems = rest[: 7 + 3 * np_], rest[7 + 3 * np_ : -1], rest[-1]
    copies = [pltpu.make_async_copy(a, b, sems.at[k]) for k, (a, b) in enumerate(zip(given, held))]
    for copy in copies:
        copy.start()
    (cells_ref, relax_ref, weight_ref, slow_ref, amp_ref, buoy_ref, mu_ref, kappa_ref, at_ref, w_ref, v_ref, bm_ref,
     sm_ref) = held
    y_refs = outs[:2]
    x_refs = outs[2 : 2 + np_]
    d_refs = outs[2 + np_ : 2 + 3 * np_]
    pulse_ref, coef_ref, base_ref, zsum_ref, z1_ref = outs[2 + 3 * np_ :]
    i, j = lax.axis_index("gx"), lax.axis_index("gy")
    rows = cx * TILE[0]
    slots = cells_ref.shape[2]
    copies[0].wait()
    cells = cells_ref[0]
    slot = lax.broadcasted_iota(jnp.int32, (1, slots), 1)
    live = slot < count_ref[0, 0]
    row_id = jnp.where(live, cells >> 7, -1)
    lane_id = cells & (TILE[1] - 1)
    wide = lax.broadcasted_iota(jnp.int32, (rows, slots), 0)
    hot_row = jnp.where(wide == row_id, 1.0, 0.0).astype(jnp.bfloat16)
    deep = lax.broadcasted_iota(jnp.int32, (TILE[1], slots), 0)
    hot_lane = jnp.where(deep == lane_id, 1.0, 0.0).astype(jnp.bfloat16)
    mask = lax.dot_general(
        hot_row, hot_lane, (((1,), (1,)), ((), ())), preferred_element_type=jnp.float32
    )
    mask = mask.reshape(cx, TILE[0], TILE[1])

    for copy in copies[1:]:
        copy.wait()
    decay, gain = decay_gain(relax_ref, weight_ref)
    for l in range(3):
        coef_ref[l] = decay[l]
        coef_ref[3 + l] = gain[l]
        coef_ref[6 + l] = jnp.full(TILE, amp_ref[0, l], jnp.float32)
    phase = wave_phase(slow_ref, onset_ref, counts)
    row = row_of()
    keep = ((row >> 2) ^ (j & 1)) == 1
    two_three = (row == 2) | (row == 3)
    four_five = (row == 4) | (row == 5)

    def pair(first, second):
        return jnp.where(
            two_three, roll(second, 2, 0), jnp.where(four_five, roll(second, -2, 0), first)
        )

    for x in range(cx):
        w = [w_ref[0, c, x] for c in range(3)]
        kappa, mu, atten = kappa_ref[x], mu_ref[x], at_ref[x]
        bb = DT2 * buoy_ref[x]
        bbmu = bb * mu
        pulse = pulse_of(-phase(x)) * mask[x]
        pulse_ref[x] = pulse_of(TIME_STEP - phase(x)) * mask[x]
        base = []
        for c in range(3):
            total = sm_ref[0, 0, c, x] + sm_ref[0, 1, c, x] + sm_ref[0, 2, c, x]
            value = 2.0 * w[c] - v_ref[0, c, x] + bb * (amp_ref[0, c] * pulse - total)
            base_ref[c, x] = value
            base.append(value)
        bm = [bm_ref[0, l, x] for l in range(3)]
        zsum = bm[0] + bm[1] + bm[2]
        z1 = decay[0] * bm[0] + decay[1] * bm[1] + decay[2] * bm[2]
        zsum_ref[x] = zsum
        z1_ref[x] = z1
        third = jnp.where(
            row == 2,
            roll(z1, 2, 0),
            jnp.where(
                row == 3,
                roll(atten, 3, 0),
                jnp.where(row == 4, roll(atten, -3, 0), jnp.where(row == 5, roll(z1, -2, 0), bbmu)),
            ),
        )
        tiles = [
            (w[0], w[1]),
            (w[2], kappa),
            (zsum, third),
            (pair(base[0], base[1]), pair(base[2], bb)),
        ]
        for t, (a, b) in enumerate(tiles):
            b = roll(b, 4, 0)
            y_refs[0][t, x] = jnp.where(keep, a, b)
            y_refs[1][t, x] = jnp.where(keep, b, a)

    for p in range(np_):
        for (name, d), at in X_AT.items():
            x = jnp.where(((i ^ p) & 1) == 0, cx - d, d - 1)
            if name[0] == "w":
                value = w_ref[0, "xyz".index(name[1]), x]
            elif name == "kappa":
                value = kappa_ref[x]
            elif name == "zsum":
                value = zsum_ref[x]
            elif name == "z1":
                value = z1_ref[x]
            elif name == "atten":
                value = at_ref[x]
            elif name == "bb":
                value = DT2 * buoy_ref[x]
            elif name == "bbmu":
                value = DT2 * buoy_ref[x] * mu_ref[x]
            else:
                value = base_ref[int(name[4]), x]
            x_refs[p][at] = value
        for q in range(2):
            for at, (t, d) in enumerate(D_LIST):
                x = jnp.where(((i ^ p) & 1) == 0, cx - d, d - 1)
                d_refs[2 * p + q][at] = y_refs[q][t, x]


def first_kernel(
    counts, np_, w_ref, kappa_ref, mu_ref, buoy_ref, at_ref, strain_ref, coef_ref, base_ref, zsum_ref,
    z1_ref, *rest,
):
    nx, ny, cx = counts
    y_refs = rest[:2]
    x_refs = rest[2 : 2 + np_]
    d_refs = rest[2 + np_ : 2 + 3 * np_]
    (term_ref, w1_ref, d0_ref, l0_ref, d1_ref, l1_ref, pb_ref, ph_ref) = rest[2 + 3 * np_ : 10 + 3 * np_]
    (side_ref, halo_ref, p0b, p0h, d0b, d0h, w1b, w1h) = rest[10 + 3 * np_ :]
    i, j = lax.axis_index("gx"), lax.axis_index("gy")
    row = row_of()

    n = len(X_LIST)
    low_there, high_there = i > 0, i < nx - 1
    even = (i & 1) == 0

    def from_sides(pick):
        if np_ == 1:
            value = pick(0)
            return value, value
        first, second = pick(0), pick(1)
        return jnp.where(even, second, first), jnp.where(even, first, second)

    for at in range(n):
        low, high = from_sides(lambda p: x_refs[p][at])
        side_ref[at] = jnp.where(low_there, low, 0.0)
        side_ref[n + at] = jnp.where(high_there, high, 0.0)

    there = jnp.where(row < 4, (j < ny - 1).astype(jnp.int32), (j > 0).astype(jnp.int32))
    mine = (row >> 2) ^ (j & 1)
    pick0, pick1 = jnp.where(mine == 0, there, 0), jnp.where(mine == 1, there, 0)
    swap0, swap1 = roll(pick0, 4, 0), roll(pick1, 4, 0)

    def unpack(t, x, r0, r1, ok):
        if ok is not None:
            r0, r1 = jnp.where(ok, r0, 0.0), jnp.where(ok, r1, 0.0)
        a = jnp.where(pick0 == 1, r0, jnp.where(pick1 == 1, r1, 0.0))
        b = roll(jnp.where(swap0 == 1, r0, jnp.where(swap1 == 1, r1, 0.0)), 4, 0)

        def second(f, near, far):
            return jnp.where(row < 4, roll(f, -near, 0), roll(f, far, 0))

        if t == 0:
            put(("wx", x), a)
            put(("wy", x), b)
        elif t == 1:
            put(("wz", x), a)
            put(("kappa", x), b)
        elif t == 2:
            put(("zsum", x), a)
            if -2 < x < cx + 1:
                put(("bbmu", x), b)
            if 0 <= x < cx:
                put(("z1", x), second(b, 2, 2))
                put(("atten", x), second(b, 3, 3))
        else:
            put(("base0", x), a)
            put(("base1", x), second(a, 2, 2))
            put(("base2", x), b)
            put(("bb", x), second(b, 2, 2))

    names = ["wx", "wy", "wz", "kappa", "zsum", "bbmu", "z1", "atten", "base0", "base1", "base2", "bb"]

    def put(key, value):
        halo_ref[names.index(key[0]), 3 + key[1]] = value

    def halo(name, x):
        return halo_ref[names.index(name), 3 + x]

    for x in range(cx):
        for t in range(4):
            unpack(t, x, y_refs[0][t, x], y_refs[1][t, x], None)
    for at, (t, d) in enumerate(D_LIST):
        low0, high0 = from_sides(lambda p: d_refs[2 * p][at])
        low1, high1 = from_sides(lambda p: d_refs[2 * p + 1][at])
        unpack(t, -d, low0, low1, low_there)
        unpack(t, cx - 1 + d, high0, high1, high_there)

    def block(name, x):
        if x < 0:
            return side_ref[X_AT[(name, -x)]]
        if x >= cx:
            return side_ref[n + X_AT[(name, x - cx + 1)]]
        if name[0] == "w":
            return w_ref[0, "xyz".index(name[1]), x]
        if name == "kappa":
            return kappa_ref[x]
        if name == "zsum":
            return zsum_ref[x]
        if name == "z1":
            return z1_ref[x]
        if name == "atten":
            return at_ref[x]
        if name == "bb":
            return DT2 * buoy_ref[x]
        if name == "bbmu":
            return DT2 * buoy_ref[x] * mu_ref[x]
        return base_ref[int(name[4]), x]

    def divergence(get_b, get_h, x, with_halo):
        yb, yh = get_b(1, x), get_h(1, x)
        up, down = yplus(yb, yh), yminus(yb, yh)
        z = get_b(2, x)
        db = 0.5 * (get_b(0, x + 1) - get_b(0, x - 1) + (up[0] - down[0]) + (zplus(z) - zminus(z)))
        if not with_halo:
            return db, None
        z = get_h(2, x)
        dh = 0.5 * (get_h(0, x + 1) - get_h(0, x - 1) + (up[1] - down[1]) + (zplus(z) - zminus(z)))
        return db, dh

    def w_b(c, x):
        return block("w" + "xyz"[c], x)

    def w_h(c, x):
        return halo("w" + "xyz"[c], x)

    for x in range(-3, cx + 3):
        inner = -3 < x < cx + 2
        db, dh = divergence(w_b, w_h, x, inner)
        p0b[3 + x] = block("kappa", x) * db - block("zsum", x)
        if -2 < x < cx + 1:
            d0b[1 + x] = db
        if inner:
            p0h[2 + x] = halo("kappa", x) * dh - halo("zsum", x)
            if 0 <= x < cx:
                d0h[x] = dh
                d0_ref[x] = db

    def lap(get_b, get_h, c, x, with_halo):
        b, h = get_b(c, x), get_h(c, x)
        up, down = yplus(b, h), yminus(b, h)
        lb = get_b(c, x + 1) + get_b(c, x - 1) + (up[0] + down[0]) + (zplus(b) + zminus(b)) - 6.0 * b
        if not with_halo:
            return lb, None
        lh = get_h(c, x + 1) + get_h(c, x - 1) + (up[1] + down[1]) + (zplus(h) + zminus(h)) - 6.0 * h
        return lb, lh

    for x in range(-2, cx + 2):
        near = -2 < x < cx + 1
        inside = 0 <= x < cx
        bb, bbmu = block("bb", x), block("bbmu", x)
        if near:
            pb, ph = p0b[3 + x], p0h[2 + x]
            up, down = yplus(pb, ph), yminus(pb, ph)
            grad_b = [0.5 * (p0b[4 + x] - p0b[2 + x]), 0.5 * (up[0] - down[0]), 0.5 * (zplus(pb) - zminus(pb))]
            grad_h = [0.5 * (p0h[3 + x] - p0h[1 + x]), 0.5 * (up[1] - down[1]), 0.5 * (zplus(ph) - zminus(ph))]
            hbb, hbbmu = halo("bb", x), halo("bbmu", x)
        else:
            grad_b = [0.5 * (p0b[4 + x] - p0b[2 + x])]
        for c in range(3 if near else 1):
            with_halo = inside or (near and c < 2)
            lb, lh = lap(w_b, w_h, c, x, with_halo)
            value = block(f"base{c}", x) + bb * grad_b[c] + bbmu * lb
            w1b[c, 2 + x] = value
            if inside:
                l0_ref[c, x] = lb
                w1_ref[0, c, x] = value
            if with_halo:
                w1h[c, 1 + x] = halo(f"base{c}", x) + hbb * grad_h[c] + hbbmu * lh

    def w1_b(c, x):
        return w1b[c, 2 + x]

    def w1_h(c, x):
        return w1h[c, 1 + x]

    gains = coef_ref[3] + coef_ref[4] + coef_ref[5]
    for x in range(-1, cx + 1):
        inside = 0 <= x < cx
        db, dh = divergence(w1_b, w1_h, x, inside)
        kappa = block("kappa", x)
        stress = kappa * db
        pb_ref[1 + x] = stress - (block("z1", x) + gains * (block("atten", x) * kappa * d0b[1 + x]))
        if not inside:
            continue
        hk = halo("kappa", x)
        ph_ref[x] = hk * dh - (halo("z1", x) + gains * (halo("atten", x) * hk * d0h[x]))
        d1_ref[x] = db
        term_ref[0, x] = kappa * d0b[1 + x] * strain_ref[0, 0, 0, x] + stress * strain_ref[0, 1, 0, x]
        total0, total1 = None, None
        for c in range(3):
            lb, _ = lap(w1_b, w1_h, c, x, False)
            l1_ref[c, x] = lb
            part0 = l0_ref[c, x] * strain_ref[0, 0, 1 + c, x]
            part1 = lb * strain_ref[0, 1, 1 + c, x]
            total0 = part0 if total0 is None else total0 + part0
            total1 = part1 if total1 is None else total1 + part1
        mu = mu_ref[x]
        term_ref[1, x] = mu * total0 + mu * total1


def last_kernel(
    counts, w_ref, bm_ref, sm_ref, kappa_ref, mu_ref, buoy_ref, bat_ref, sat_ref, coef_ref, pulse_ref, w1_ref, d0_ref, l0_ref, d1_ref, l1_ref, pb_ref, ph_ref, w2_ref, bn_ref, sn_ref,
):
    nx, ny, cx = counts
    decay, gain, amp = ([coef_ref[3 * k + l] for l in range(3)] for k in range(3))
    for x in range(cx):
        bulk = bat_ref[x] * kappa_ref[x]
        q0, q1 = bulk * d0_ref[x], bulk * d1_ref[x]
        for l in range(3):
            now = decay[l] * bm_ref[0, l, x] + gain[l] * q0
            bn_ref[0, l, x] = decay[l] * now + gain[l] * q1
        pb = pb_ref[1 + x]
        ph = ph_ref[x]
        up, down = yplus(pb, ph), yminus(pb, ph)
        grad = [
            0.5 * (pb_ref[2 + x] - pb_ref[x]),
            0.5 * (up[0] - down[0]),
            0.5 * (zplus(pb) - zminus(pb)),
        ]
        mu = mu_ref[x]
        shear = sat_ref[x] * mu
        pulse = pulse_ref[x]
        bb = DT2 * buoy_ref[x]
        for c in range(3):
            l1 = l1_ref[c, x]
            q0, q1 = shear * l0_ref[c, x], shear * l1
            total = None
            for l in range(3):
                now = decay[l] * sm_ref[0, l, c, x] + gain[l] * q0
                sn_ref[0, l, c, x] = decay[l] * now + gain[l] * q1
                total = now if total is None else total + now
            force = grad[c] + mu * l1 - total + amp[c] * pulse
            w2_ref[0, c, x] = 2.0 * w1_ref[0, c, x] - w_ref[0, c, x] + bb * force


def matched(value, mesh_shape, along_x, along_y, p, q):
    nx, ny = mesh_shape
    pairs = []
    for a in range(nx):
        for b in range(ny):
            c, d = a, b
            if along_x:
                c = a + 1 if a % 2 == p else a - 1
            if along_y:
                d = b + 1 if b % 2 == q else b - 1
            if not (0 <= c < nx and 0 <= d < ny):
                c, d = a, b
            pairs.append((a * ny + b, c * ny + d))
    return lax.ppermute(value, ("gx", "gy"), pairs)


def event_sum(value):
    count = lax.axis_size("event")
    if count & (count - 1):
        return lax.psum(value, "event")
    step = 1
    while step < count:
        value = value + lax.ppermute(value, "event", [(e, e ^ step) for e in range(count)])
        step *= 2
    return value


def vmem():
    return pl.BlockSpec(memory_space=pltpu.VMEM)


def body(
    adjoint_now, adjoint_old, bulk_memory, shear_memory, forward_strain, bulk_modulus, shear_modulus, buoyancy,
    bulk_atten, shear_atten, relax_time, mechanism_weight, event_slowness, event_amplitude, event_onset,
    boundary_cells, boundary_count,
):
    nx, ny = lax.axis_size("gx"), lax.axis_size("gy")
    cx = bulk_modulus.shape[0]
    counts = (nx, ny, cx)
    np_ = 1 if nx == 2 else 2
    f32 = jnp.float32

    def field(*lead):
        return jax.ShapeDtypeStruct((*lead, *TILE), f32)

    params = pltpu.CompilerParams(vmem_limit_bytes=24 * 1024 * 1024)
    pack_args = (
        boundary_count, event_onset, boundary_cells, relax_time, mechanism_weight, event_slowness, event_amplitude,
        buoyancy, shear_modulus, bulk_modulus, bulk_atten, adjoint_now, adjoint_old, bulk_memory, shear_memory,
    )
    packed = pl.pallas_call(
        functools.partial(pack_kernel, counts, np_),
        out_shape=[field(4, cx)] * 2
        + [field(len(X_LIST))] * np_
        + [field(len(D_LIST))] * (2 * np_)
        + [field(cx), field(9), field(3, cx), field(cx), field(cx)],
        in_specs=[
            pl.BlockSpec(memory_space=pltpu.HBM if given.size > 1 else pltpu.SMEM) for given in pack_args
        ],
        out_specs=[vmem()] * (2 + 3 * np_ + 5),
        scratch_shapes=[
            (pltpu.SMEM if k in (1, 2, 3, 4) else pltpu.VMEM)(given.shape, given.dtype)
            for k, given in enumerate(pack_args[2:])
        ]
        + [pltpu.SemaphoreType.DMA((PACK_ARGS - 2,))],
        compiler_params=params,
        name="pack",
    )(
        *(
            pltpu.with_memory_space_constraint(given, pltpu.HBM) if given.size > 1 else given
            for given in pack_args
        )
    )
    shape = (nx, ny)
    ys = [matched(packed[q], shape, False, True, 0, q) for q in range(2)]
    xs = [matched(packed[2 + p], shape, True, False, p, 0) for p in range(np_)]
    ds = [
        matched(packed[2 + np_ + 2 * p + q], shape, True, True, p, q) for p in range(np_) for q in range(2)
    ]
    pulse, coef, base, zsum, z1 = packed[2 + 3 * np_ :]

    first = pl.pallas_call(
        functools.partial(first_kernel, counts, np_),
        out_shape=[
            field(2, cx), field(1, 3, cx), field(cx), field(3, cx), field(cx), field(3, cx), field(cx + 2), field(cx),
        ],
        in_specs=[vmem()] * (12 + 3 * np_),
        out_specs=[vmem()] * 8,
        scratch_shapes=[
            pltpu.VMEM((2 * len(X_LIST), *TILE), f32),
            pltpu.VMEM((12, cx + 6, *TILE), f32),
            pltpu.VMEM((cx + 6, *TILE), f32),
            pltpu.VMEM((cx + 4, *TILE), f32),
            pltpu.VMEM((cx + 2, *TILE), f32),
            pltpu.VMEM((cx, *TILE), f32),
            pltpu.VMEM((3, cx + 4, *TILE), f32),
            pltpu.VMEM((3, cx + 2, *TILE), f32),
        ],
        compiler_params=params,
        name="first",
    )(
        adjoint_now, bulk_modulus, shear_modulus, buoyancy, bulk_atten, forward_strain, coef, base, zsum, z1, *ys, *xs, *ds,
    )
    term, w1, d0, l0, d1, l1, pb, ph = first
    total = event_sum(term)

    w2, bulk_next, shear_next = pl.pallas_call(
        functools.partial(last_kernel, counts),
        out_shape=[field(1, 3, cx), field(1, 3, cx), field(1, 3, 3, cx)],
        in_specs=[vmem()] * 17,
        out_specs=[vmem()] * 3,
        compiler_params=params,
        cost_estimate=pl.CostEstimate(flops=3_000_000, bytes_accessed=4_000_000, transcendentals=0),
        name="last",
    )(
        adjoint_now, bulk_memory, shear_memory, bulk_modulus, shear_modulus, buoyancy, bulk_atten, shear_atten,
        coef, pulse, w1, d0, l0, d1, l1, pb, ph,
    )
    return w2, w1, bulk_next, shear_next, total[0], total[1]


def solution(mesh):
    wide = P("event", None, "gx", "gy", None)
    wider = P("event", None, None, "gx", "gy", None)
    grid = P("gx", "gy", None)
    return jax.shard_map(
        body,
        mesh=mesh,
        in_specs=(
            wide, wide, wide, wider, wider, grid, grid, grid, grid, grid, P(), P(), P("event", None),
            P("event", None), P("event"), grid, P("gx", "gy"),
        ),
        out_specs=(wide, wide, wide, wider, grid, grid),
        check_vma=False,
    )
```

```python
import functools

import jax
import jax.numpy as jnp
from jax import lax
from jax.experimental import pallas as pl
from jax.experimental.pallas import tpu as pltpu
from jax.sharding import PartitionSpec as P

TIME_STEP = 0.3
DT2 = TIME_STEP * TIME_STEP
TILE = (8, 128)

X_LIST = (
    [("wx", d) for d in (1, 2, 3, 4)]
    + [("wy", d) for d in (1, 2, 3)]
    + [("wz", d) for d in (1, 2, 3)]
    + [("kappa", d) for d in (1, 2, 3)]
    + [("zsum", d) for d in (1, 2, 3)]
    + [(f"base{c}", d) for c in range(3) for d in (1, 2)]
    + [("bb", d) for d in (1, 2)]
    + [("bbmu", d) for d in (1, 2)]
    + [("z1", 1), ("atten", 1)]
)
X_AT = {key: at for at, key in enumerate(X_LIST)}
PACK_ARGS = 15
D_LIST = [(t, 1) for t in range(4)] + [(t, 2) for t in range(3)] + [(0, 3)]


def roll(tile, shift, axis):
    return pltpu.roll(tile, shift % TILE[axis], axis)


def row_of():
    return lax.broadcasted_iota(jnp.int32, TILE, 0)


def lane_of():
    return lax.broadcasted_iota(jnp.int32, TILE, 1)


def zplus(f):
    return jnp.where(lane_of() == TILE[1] - 1, 0.0, roll(f, -1, 1))


def zminus(f):
    return jnp.where(lane_of() == 0, 0.0, roll(f, 1, 1))


def yplus(block, halo):
    b, h = roll(block, -1, 0), roll(halo, -1, 0)
    last = row_of() == TILE[0] - 1
    return jnp.where(last, h, b), jnp.where(last, b, h)


def yminus(block, halo):
    b, h = roll(block, 1, 0), roll(halo, 1, 0)
    first = row_of() == 0
    return jnp.where(first, h, b), jnp.where(first, b, h)


def decay_gain(relax_ref, weight_ref):
    decay, gain = [], []
    for l in range(relax_ref.shape[0]):
        d = jnp.exp(-TIME_STEP / jnp.full(TILE, relax_ref[l], jnp.float32))
        decay.append(d)
        gain.append((1.0 - d) * weight_ref[l])
    return decay, gain


def wave_phase(slow_ref, onset_ref, counts):
    nx, ny, cx = counts
    i, j = lax.axis_index("gx"), lax.axis_index("gy")
    py = (j * TILE[0] + row_of()).astype(jnp.float32) / float(ny * TILE[0])
    pz = lane_of().astype(jnp.float32) / float(TILE[1])
    common = slow_ref[0, 1] * py + slow_ref[0, 2] * pz + onset_ref[0]

    def at(x):
        px = jnp.full(TILE, i * cx + x, jnp.int32).astype(jnp.float32) / float(nx * cx)
        return slow_ref[0, 0] * px + common

    return at


def pulse_of(tau):
    square = tau * tau
    return (1.0 - 2.0 * square) * jnp.exp(-square)


def pack_kernel(
    counts, np_, *refs,
):
    nx, ny, cx = counts
    count_ref, onset_ref, given, rest = refs[0], refs[1], refs[2:PACK_ARGS], refs[PACK_ARGS:]
    outs, held, sems = rest[: 7 + 3 * np_], rest[7 + 3 * np_ : -1], rest[-1]
    copies = [pltpu.make_async_copy(a, b, sems.at[k]) for k, (a, b) in enumerate(zip(given, held))]
    for copy in copies:
        copy.start()
    (cells_ref, relax_ref, weight_ref, slow_ref, amp_ref, buoy_ref, mu_ref, kappa_ref, at_ref, w_ref, v_ref, bm_ref,
     sm_ref) = held
    y_refs = outs[:2]
    x_refs = outs[2 : 2 + np_]
    d_refs = outs[2 + np_ : 2 + 3 * np_]
    pulse_ref, coef_ref, base_ref, zsum_ref, z1_ref = outs[2 + 3 * np_ :]
    i, j = lax.axis_index("gx"), lax.axis_index("gy")
    rows = cx * TILE[0]
    slots = cells_ref.shape[2]
    copies[0].wait()
    cells = cells_ref[0]
    slot = lax.broadcasted_iota(jnp.int32, (1, slots), 1)
    live = slot < count_ref[0, 0]
    row_id = jnp.where(live, cells >> 7, -1)
    lane_id = cells & (TILE[1] - 1)
    wide = lax.broadcasted_iota(jnp.int32, (rows, slots), 0)
    hot_row = jnp.where(wide == row_id, 1.0, 0.0).astype(jnp.bfloat16)
    deep = lax.broadcasted_iota(jnp.int32, (TILE[1], slots), 0)
    hot_lane = jnp.where(deep == lane_id, 1.0, 0.0).astype(jnp.bfloat16)
    mask = lax.dot_general(
        hot_row, hot_lane, (((1,), (1,)), ((), ())), preferred_element_type=jnp.float32
    )
    mask = mask.reshape(cx, TILE[0], TILE[1])

    for copy in copies[1:]:
        copy.wait()
    decay, gain = decay_gain(relax_ref, weight_ref)
    for l in range(3):
        coef_ref[l] = decay[l]
        coef_ref[3 + l] = gain[l]
        coef_ref[6 + l] = jnp.full(TILE, amp_ref[0, l], jnp.float32)
    phase = wave_phase(slow_ref, onset_ref, counts)
    row = row_of()
    keep = ((row >> 2) ^ (j & 1)) == 1
    two_three = (row == 2) | (row == 3)
    four_five = (row == 4) | (row == 5)

    def pair(first, second):
        return jnp.where(
            two_three, roll(second, 2, 0), jnp.where(four_five, roll(second, -2, 0), first)
        )

    for x in range(cx):
        w = [w_ref[0, c, x] for c in range(3)]
        kappa, mu, atten = kappa_ref[x], mu_ref[x], at_ref[x]
        bb = DT2 * buoy_ref[x]
        bbmu = bb * mu
        pulse = pulse_of(-phase(x)) * mask[x]
        pulse_ref[x] = pulse_of(TIME_STEP - phase(x)) * mask[x]
        base = []
        for c in range(3):
            total = sm_ref[0, 0, c, x] + sm_ref[0, 1, c, x] + sm_ref[0, 2, c, x]
            value = 2.0 * w[c] - v_ref[0, c, x] + bb * (amp_ref[0, c] * pulse - total)
            base_ref[c, x] = value
            base.append(value)
        bm = [bm_ref[0, l, x] for l in range(3)]
        zsum = bm[0] + bm[1] + bm[2]
        z1 = decay[0] * bm[0] + decay[1] * bm[1] + decay[2] * bm[2]
        zsum_ref[x] = zsum
        z1_ref[x] = z1
        third = jnp.where(
            row == 2,
            roll(z1, 2, 0),
            jnp.where(
                row == 3,
                roll(atten, 3, 0),
                jnp.where(row == 4, roll(atten, -3, 0), jnp.where(row == 5, roll(z1, -2, 0), bbmu)),
            ),
        )
        tiles = [
            (w[0], w[1]),
            (w[2], kappa),
            (zsum, third),
            (pair(base[0], base[1]), pair(base[2], bb)),
        ]
        for t, (a, b) in enumerate(tiles):
            b = roll(b, 4, 0)
            y_refs[0][t, x] = jnp.where(keep, a, b)
            y_refs[1][t, x] = jnp.where(keep, b, a)

    for p in range(np_):
        for (name, d), at in X_AT.items():
            x = jnp.where(((i ^ p) & 1) == 0, cx - d, d - 1)
            if name[0] == "w":
                value = w_ref[0, "xyz".index(name[1]), x]
            elif name == "kappa":
                value = kappa_ref[x]
            elif name == "zsum":
                value = zsum_ref[x]
            elif name == "z1":
                value = z1_ref[x]
            elif name == "atten":
                value = at_ref[x]
            elif name == "bb":
                value = DT2 * buoy_ref[x]
            elif name == "bbmu":
                value = DT2 * buoy_ref[x] * mu_ref[x]
            else:
                value = base_ref[int(name[4]), x]
            x_refs[p][at] = value
        for q in range(2):
            for at, (t, d) in enumerate(D_LIST):
                x = jnp.where(((i ^ p) & 1) == 0, cx - d, d - 1)
                d_refs[2 * p + q][at] = y_refs[q][t, x]


def first_kernel(
    counts, np_, w_ref, kappa_ref, mu_ref, buoy_ref, at_ref, strain_ref, coef_ref, base_ref, zsum_ref,
    z1_ref, *rest,
):
    nx, ny, cx = counts
    y_refs = rest[:2]
    x_refs = rest[2 : 2 + np_]
    d_refs = rest[2 + np_ : 2 + 3 * np_]
    (term_ref, w1_ref, d0_ref, l0_ref, d1_ref, l1_ref, pb_ref, ph_ref) = rest[2 + 3 * np_ : 10 + 3 * np_]
    (side_ref, halo_ref, p0b, p0h, d0b, d0h, w1b, w1h) = rest[10 + 3 * np_ :]
    i, j = lax.axis_index("gx"), lax.axis_index("gy")
    row = row_of()

    n = len(X_LIST)
    low_there, high_there = i > 0, i < nx - 1
    even = (i & 1) == 0

    def from_sides(pick):
        if np_ == 1:
            value = pick(0)
            return value, value
        first, second = pick(0), pick(1)
        return jnp.where(even, second, first), jnp.where(even, first, second)

    for at in range(n):
        low, high = from_sides(lambda p: x_refs[p][at])
        side_ref[at] = jnp.where(low_there, low, 0.0)
        side_ref[n + at] = jnp.where(high_there, high, 0.0)

    there = jnp.where(row < 4, (j < ny - 1).astype(jnp.int32), (j > 0).astype(jnp.int32))
    mine = (row >> 2) ^ (j & 1)
    pick0, pick1 = jnp.where(mine == 0, there, 0), jnp.where(mine == 1, there, 0)
    swap0, swap1 = roll(pick0, 4, 0), roll(pick1, 4, 0)

    def unpack(t, x, r0, r1, ok):
        if ok is not None:
            r0, r1 = jnp.where(ok, r0, 0.0), jnp.where(ok, r1, 0.0)
        a = jnp.where(pick0 == 1, r0, jnp.where(pick1 == 1, r1, 0.0))
        b = roll(jnp.where(swap0 == 1, r0, jnp.where(swap1 == 1, r1, 0.0)), 4, 0)

        def second(f, near, far):
            return jnp.where(row < 4, roll(f, -near, 0), roll(f, far, 0))

        if t == 0:
            put(("wx", x), a)
            put(("wy", x), b)
        elif t == 1:
            put(("wz", x), a)
            put(("kappa", x), b)
        elif t == 2:
            put(("zsum", x), a)
            if -2 < x < cx + 1:
                put(("bbmu", x), b)
            if 0 <= x < cx:
                put(("z1", x), second(b, 2, 2))
                put(("atten", x), second(b, 3, 3))
        else:
            put(("base0", x), a)
            put(("base1", x), second(a, 2, 2))
            put(("base2", x), b)
            put(("bb", x), second(b, 2, 2))

    names = ["wx", "wy", "wz", "kappa", "zsum", "bbmu", "z1", "atten", "base0", "base1", "base2", "bb"]

    def put(key, value):
        halo_ref[names.index(key[0]), 3 + key[1]] = value

    def halo(name, x):
        return halo_ref[names.index(name), 3 + x]

    for x in range(cx):
        for t in range(4):
            unpack(t, x, y_refs[0][t, x], y_refs[1][t, x], None)
    for at, (t, d) in enumerate(D_LIST):
        low0, high0 = from_sides(lambda p: d_refs[2 * p][at])
        low1, high1 = from_sides(lambda p: d_refs[2 * p + 1][at])
        unpack(t, -d, low0, low1, low_there)
        unpack(t, cx - 1 + d, high0, high1, high_there)

    def block(name, x):
        if x < 0:
            return side_ref[X_AT[(name, -x)]]
        if x >= cx:
            return side_ref[n + X_AT[(name, x - cx + 1)]]
        if name[0] == "w":
            return w_ref[0, "xyz".index(name[1]), x]
        if name == "kappa":
            return kappa_ref[x]
        if name == "zsum":
            return zsum_ref[x]
        if name == "z1":
            return z1_ref[x]
        if name == "atten":
            return at_ref[x]
        if name == "bb":
            return DT2 * buoy_ref[x]
        if name == "bbmu":
            return DT2 * buoy_ref[x] * mu_ref[x]
        return base_ref[int(name[4]), x]

    def divergence(get_b, get_h, x, with_halo):
        yb, yh = get_b(1, x), get_h(1, x)
        up, down = yplus(yb, yh), yminus(yb, yh)
        z = get_b(2, x)
        db = 0.5 * (get_b(0, x + 1) - get_b(0, x - 1) + (up[0] - down[0]) + (zplus(z) - zminus(z)))
        if not with_halo:
            return db, None
        z = get_h(2, x)
        dh = 0.5 * (get_h(0, x + 1) - get_h(0, x - 1) + (up[1] - down[1]) + (zplus(z) - zminus(z)))
        return db, dh

    def w_b(c, x):
        return block("w" + "xyz"[c], x)

    def w_h(c, x):
        return halo("w" + "xyz"[c], x)

    for x in range(-3, cx + 3):
        inner = -3 < x < cx + 2
        db, dh = divergence(w_b, w_h, x, inner)
        p0b[3 + x] = block("kappa", x) * db - block("zsum", x)
        if -2 < x < cx + 1:
            d0b[1 + x] = db
        if inner:
            p0h[2 + x] = halo("kappa", x) * dh - halo("zsum", x)
            if 0 <= x < cx:
                d0h[x] = dh
                d0_ref[x] = db

    def lap(get_b, get_h, c, x, with_halo):
        b, h = get_b(c, x), get_h(c, x)
        up, down = yplus(b, h), yminus(b, h)
        lb = get_b(c, x + 1) + get_b(c, x - 1) + (up[0] + down[0]) + (zplus(b) + zminus(b)) - 6.0 * b
        if not with_halo:
            return lb, None
        lh = get_h(c, x + 1) + get_h(c, x - 1) + (up[1] + down[1]) + (zplus(h) + zminus(h)) - 6.0 * h
        return lb, lh

    for x in range(-2, cx + 2):
        near = -2 < x < cx + 1
        inside = 0 <= x < cx
        bb, bbmu = block("bb", x), block("bbmu", x)
        if near:
            pb, ph = p0b[3 + x], p0h[2 + x]
            up, down = yplus(pb, ph), yminus(pb, ph)
            grad_b = [0.5 * (p0b[4 + x] - p0b[2 + x]), 0.5 * (up[0] - down[0]), 0.5 * (zplus(pb) - zminus(pb))]
            grad_h = [0.5 * (p0h[3 + x] - p0h[1 + x]), 0.5 * (up[1] - down[1]), 0.5 * (zplus(ph) - zminus(ph))]
            hbb, hbbmu = halo("bb", x), halo("bbmu", x)
        else:
            grad_b = [0.5 * (p0b[4 + x] - p0b[2 + x])]
        for c in range(3 if near else 1):
            with_halo = inside or (near and c < 2)
            lb, lh = lap(w_b, w_h, c, x, with_halo)
            value = block(f"base{c}", x) + bb * grad_b[c] + bbmu * lb
            w1b[c, 2 + x] = value
            if inside:
                l0_ref[c, x] = lb
                w1_ref[c, x] = value
            if with_halo:
                w1h[c, 1 + x] = halo(f"base{c}", x) + hbb * grad_h[c] + hbbmu * lh

    def w1_b(c, x):
        return w1b[c, 2 + x]

    def w1_h(c, x):
        return w1h[c, 1 + x]

    gains = coef_ref[3] + coef_ref[4] + coef_ref[5]
    for x in range(-1, cx + 1):
        inside = 0 <= x < cx
        db, dh = divergence(w1_b, w1_h, x, inside)
        kappa = block("kappa", x)
        stress = kappa * db
        pb_ref[1 + x] = stress - (block("z1", x) + gains * (block("atten", x) * kappa * d0b[1 + x]))
        if not inside:
            continue
        hk = halo("kappa", x)
        ph_ref[x] = hk * dh - (halo("z1", x) + gains * (halo("atten", x) * hk * d0h[x]))
        d1_ref[x] = db
        term_ref[0, x] = kappa * d0b[1 + x] * strain_ref[0, 0, 0, x] + stress * strain_ref[0, 1, 0, x]
        total0, total1 = None, None
        for c in range(3):
            lb, _ = lap(w1_b, w1_h, c, x, False)
            l1_ref[c, x] = lb
            part0 = l0_ref[c, x] * strain_ref[0, 0, 1 + c, x]
            part1 = lb * strain_ref[0, 1, 1 + c, x]
            total0 = part0 if total0 is None else total0 + part0
            total1 = part1 if total1 is None else total1 + part1
        mu = mu_ref[x]
        term_ref[1, x] = mu * total0 + mu * total1


def last_kernel(
    counts, w_ref, bm_ref, sm_ref, kappa_ref, mu_ref, buoy_ref, bat_ref, sat_ref, coef_ref, pulse_ref, w1_ref, d0_ref, l0_ref, d1_ref, l1_ref, pb_ref, ph_ref, w2_ref, before_ref, bn_ref, sn_ref,
):
    nx, ny, cx = counts
    decay, gain, amp = ([coef_ref[3 * k + l] for l in range(3)] for k in range(3))
    for x in range(cx):
        bulk = bat_ref[x] * kappa_ref[x]
        q0, q1 = bulk * d0_ref[x], bulk * d1_ref[x]
        for l in range(3):
            now = decay[l] * bm_ref[0, l, x] + gain[l] * q0
            bn_ref[0, l, x] = decay[l] * now + gain[l] * q1
        pb = pb_ref[1 + x]
        ph = ph_ref[x]
        up, down = yplus(pb, ph), yminus(pb, ph)
        grad = [
            0.5 * (pb_ref[2 + x] - pb_ref[x]),
            0.5 * (up[0] - down[0]),
            0.5 * (zplus(pb) - zminus(pb)),
        ]
        mu = mu_ref[x]
        shear = sat_ref[x] * mu
        pulse = pulse_ref[x]
        bb = DT2 * buoy_ref[x]
        for c in range(3):
            l1 = l1_ref[c, x]
            q0, q1 = shear * l0_ref[c, x], shear * l1
            total = None
            for l in range(3):
                now = decay[l] * sm_ref[0, l, c, x] + gain[l] * q0
                sn_ref[0, l, c, x] = decay[l] * now + gain[l] * q1
                total = now if total is None else total + now
            force = grad[c] + mu * l1 - total + amp[c] * pulse
            w1 = w1_ref[c, x]
            before_ref[0, c, x] = w1
            w2_ref[0, c, x] = 2.0 * w1 - w_ref[0, c, x] + bb * force


def matched(value, mesh_shape, along_x, along_y, p, q):
    nx, ny = mesh_shape
    pairs = []
    for a in range(nx):
        for b in range(ny):
            c, d = a, b
            if along_x:
                c = a + 1 if a % 2 == p else a - 1
            if along_y:
                d = b + 1 if b % 2 == q else b - 1
            if not (0 <= c < nx and 0 <= d < ny):
                c, d = a, b
            pairs.append((a * ny + b, c * ny + d))
    return lax.ppermute(value, ("gx", "gy"), pairs)


def event_sum(value):
    count = lax.axis_size("event")
    if count & (count - 1):
        return lax.psum(value, "event")
    step = 1
    while step < count:
        value = value + lax.ppermute(value, "event", [(e, e ^ step) for e in range(count)])
        step *= 2
    return value


def vmem():
    return pl.BlockSpec(memory_space=pltpu.VMEM)


def body(
    adjoint_now, adjoint_old, bulk_memory, shear_memory, forward_strain, bulk_modulus, shear_modulus, buoyancy,
    bulk_atten, shear_atten, relax_time, mechanism_weight, event_slowness, event_amplitude, event_onset,
    boundary_cells, boundary_count,
):
    nx, ny = lax.axis_size("gx"), lax.axis_size("gy")
    cx = bulk_modulus.shape[0]
    counts = (nx, ny, cx)
    np_ = 1 if nx == 2 else 2
    f32 = jnp.float32

    def field(*lead):
        return jax.ShapeDtypeStruct((*lead, *TILE), f32)

    params = pltpu.CompilerParams(vmem_limit_bytes=24 * 1024 * 1024)
    pack_args = (
        boundary_count, event_onset, boundary_cells, relax_time, mechanism_weight, event_slowness, event_amplitude,
        buoyancy, shear_modulus, bulk_modulus, bulk_atten, adjoint_now, adjoint_old, bulk_memory, shear_memory,
    )
    packed = pl.pallas_call(
        functools.partial(pack_kernel, counts, np_),
        out_shape=[field(4, cx)] * 2
        + [field(len(X_LIST))] * np_
        + [field(len(D_LIST))] * (2 * np_)
        + [field(cx), field(9), field(3, cx), field(cx), field(cx)],
        in_specs=[
            pl.BlockSpec(memory_space=pltpu.HBM if given.size > 1 else pltpu.SMEM) for given in pack_args
        ],
        out_specs=[vmem()] * (2 + 3 * np_ + 5),
        scratch_shapes=[
            (pltpu.SMEM if k in (1, 2, 3, 4) else pltpu.VMEM)(given.shape, given.dtype)
            for k, given in enumerate(pack_args[2:])
        ]
        + [pltpu.SemaphoreType.DMA((PACK_ARGS - 2,))],
        compiler_params=params,
        name="pack",
    )(
        *(
            pltpu.with_memory_space_constraint(given, pltpu.HBM) if given.size > 1 else given
            for given in pack_args
        )
    )
    shape = (nx, ny)
    ys = [matched(packed[q], shape, False, True, 0, q) for q in range(2)]
    xs = [matched(packed[2 + p], shape, True, False, p, 0) for p in range(np_)]
    ds = [
        matched(packed[2 + np_ + 2 * p + q], shape, True, True, p, q) for p in range(np_) for q in range(2)
    ]
    pulse, coef, base, zsum, z1 = packed[2 + 3 * np_ :]

    first = pl.pallas_call(
        functools.partial(first_kernel, counts, np_),
        out_shape=[
            field(2, cx), field(3, cx), field(cx), field(3, cx), field(cx), field(3, cx), field(cx + 2), field(cx),
        ],
        in_specs=[vmem()] * (12 + 3 * np_),
        out_specs=[vmem()] * 8,
        scratch_shapes=[
            pltpu.VMEM((2 * len(X_LIST), *TILE), f32),
            pltpu.VMEM((12, cx + 6, *TILE), f32),
            pltpu.VMEM((cx + 6, *TILE), f32),
            pltpu.VMEM((cx + 4, *TILE), f32),
            pltpu.VMEM((cx + 2, *TILE), f32),
            pltpu.VMEM((cx, *TILE), f32),
            pltpu.VMEM((3, cx + 4, *TILE), f32),
            pltpu.VMEM((3, cx + 2, *TILE), f32),
        ],
        compiler_params=params,
        name="first",
    )(
        adjoint_now, bulk_modulus, shear_modulus, buoyancy, bulk_atten, forward_strain, coef, base, zsum, z1, *ys, *xs, *ds,
    )
    term, w1, d0, l0, d1, l1, pb, ph = first
    total = event_sum(term)

    w2, before, bulk_next, shear_next = pl.pallas_call(
        functools.partial(last_kernel, counts),
        out_shape=[field(1, 3, cx), field(1, 3, cx), field(1, 3, cx), field(1, 3, 3, cx)],
        in_specs=[vmem()] * 17,
        out_specs=[vmem()] * 4,
        compiler_params=params,
        cost_estimate=pl.CostEstimate(flops=3_000_000, bytes_accessed=4_000_000, transcendentals=0),
        name="last",
    )(
        adjoint_now, bulk_memory, shear_memory, bulk_modulus, shear_modulus, buoyancy, bulk_atten, shear_atten,
        coef, pulse, w1, d0, l0, d1, l1, pb, ph,
    )
    return w2, before, bulk_next, shear_next, total[0], total[1]


def solution(mesh):
    wide = P("event", None, "gx", "gy", None)
    wider = P("event", None, None, "gx", "gy", None)
    grid = P("gx", "gy", None)
    return jax.shard_map(
        body,
        mesh=mesh,
        in_specs=(
            wide, wide, wide, wider, wider, grid, grid, grid, grid, grid, P(), P(), P("event", None),
            P("event", None), P("event"), grid, P("gx", "gy"),
        ),
        out_specs=(wide, wide, wide, wider, grid, grid),
        check_vma=False,
    )
```

```python
import functools

import jax
import jax.numpy as jnp
from jax import lax
from jax.experimental import pallas as pl
from jax.experimental.pallas import tpu as pltpu
from jax.sharding import PartitionSpec as P

TIME_STEP = 0.3
DT2 = TIME_STEP * TIME_STEP
TILE = (8, 128)

X_LIST = (
    [("wx", d) for d in (1, 2, 3, 4)]
    + [("wy", d) for d in (1, 2, 3)]
    + [("wz", d) for d in (1, 2, 3)]
    + [("kappa", d) for d in (1, 2, 3)]
    + [("zsum", d) for d in (1, 2, 3)]
    + [(f"base{c}", d) for c in range(3) for d in (1, 2)]
    + [("bb", d) for d in (1, 2)]
    + [("bbmu", d) for d in (1, 2)]
    + [("z1", 1), ("atten", 1), ("mask", 1), ("mask", 2)]
)
X_AT = {key: at for at, key in enumerate(X_LIST)}
PACK_ARGS = 14
D_LIST = [(t, 1) for t in range(4)] + [(t, 2) for t in range(3)] + [(0, 3)]


def roll(tile, shift, axis):
    return pltpu.roll(tile, shift % TILE[axis], axis)


def row_of():
    return lax.broadcasted_iota(jnp.int32, TILE, 0)


def lane_of():
    return lax.broadcasted_iota(jnp.int32, TILE, 1)


def zplus(f):
    return jnp.where(lane_of() == TILE[1] - 1, 0.0, roll(f, -1, 1))


def zminus(f):
    return jnp.where(lane_of() == 0, 0.0, roll(f, 1, 1))


def yplus(block, halo):
    b, h = roll(block, -1, 0), roll(halo, -1, 0)
    last = row_of() == TILE[0] - 1
    return jnp.where(last, h, b), jnp.where(last, b, h)


def yminus(block, halo):
    b, h = roll(block, 1, 0), roll(halo, 1, 0)
    first = row_of() == 0
    return jnp.where(first, h, b), jnp.where(first, b, h)


def decay_gain(relax_ref, weight_ref):
    decay, gain = [], []
    for l in range(relax_ref.shape[0]):
        d = jnp.exp(-TIME_STEP / jnp.full(TILE, relax_ref[l], jnp.float32))
        decay.append(d)
        gain.append((1.0 - d) * weight_ref[l])
    return decay, gain


def wave_phase(slow, onset_ref, counts, y):
    nx, ny, cx = counts
    i, j = lax.axis_index("gx"), lax.axis_index("gy")
    py = (j * TILE[0] + y).astype(jnp.float32) / float(ny * TILE[0])
    pz = lane_of().astype(jnp.float32) / float(TILE[1])
    common = slow[1] * py + slow[2] * pz + onset_ref[0]

    def at(x):
        px = jnp.full(TILE, i * cx + x, jnp.int32).astype(jnp.float32) / float(nx * cx)
        return slow[0] * px + common

    return at


def pulse_of(tau):
    square = tau * tau
    return (1.0 - 2.0 * square) * jnp.exp(-square)


def pack_kernel(
    counts, np_, *refs,
):
    nx, ny, cx = counts
    count_ref, given, rest = refs[0], refs[1:PACK_ARGS], refs[PACK_ARGS:]
    outs, held, sems = rest[: 7 + 3 * np_], rest[7 + 3 * np_ : -1], rest[-1]
    copies = [pltpu.make_async_copy(a, b, sems.at[k]) for k, (a, b) in enumerate(zip(given, held))]
    for copy in copies:
        copy.start()
    (cells_ref, relax_ref, weight_ref, slow_ref, amp_ref, buoy_ref, mu_ref, kappa_ref, at_ref, w_ref, v_ref, bm_ref,
     sm_ref) = held
    y_refs = outs[:2]
    x_refs = outs[2 : 2 + np_]
    d_refs = outs[2 + np_ : 2 + 3 * np_]
    mask_ref, coef_ref, base_ref, zsum_ref, z1_ref = outs[2 + 3 * np_ :]
    i, j = lax.axis_index("gx"), lax.axis_index("gy")
    rows = cx * TILE[0]
    slots = cells_ref.shape[2]
    copies[0].wait()
    cells = cells_ref[0]
    slot = lax.broadcasted_iota(jnp.int32, (1, slots), 1)
    live = slot < count_ref[0, 0]
    row_id = jnp.where(live, cells >> 7, -1)
    lane_id = cells & (TILE[1] - 1)
    wide = lax.broadcasted_iota(jnp.int32, (rows, slots), 0)
    hot_row = jnp.where(wide == row_id, 1.0, 0.0).astype(jnp.bfloat16)
    deep = lax.broadcasted_iota(jnp.int32, (TILE[1], slots), 0)
    hot_lane = jnp.where(deep == lane_id, 1.0, 0.0).astype(jnp.bfloat16)
    mask = lax.dot_general(
        hot_row, hot_lane, (((1,), (1,)), ((), ())), preferred_element_type=jnp.float32
    )
    mask_ref[...] = mask.reshape(cx, TILE[0], TILE[1])

    for copy in copies[1:]:
        copy.wait()
    decay, gain = decay_gain(relax_ref, weight_ref)
    for l in range(3):
        coef_ref[l] = decay[l]
        coef_ref[3 + l] = gain[l]
        coef_ref[6 + l] = jnp.full(TILE, amp_ref[0, l], jnp.float32)
        coef_ref[9 + l] = jnp.full(TILE, slow_ref[0, l], jnp.float32)
    row = row_of()
    keep = ((row >> 2) ^ (j & 1)) == 1
    two_three = (row == 2) | (row == 3)
    four_five = (row == 4) | (row == 5)

    def pair(first, second):
        return jnp.where(
            two_three, roll(second, 2, 0), jnp.where(four_five, roll(second, -2, 0), first)
        )

    def spare(field, live, shift):
        return jnp.where(
            row == 3, roll(live, shift, 0), jnp.where(row == 4, roll(live, -shift, 0), field)
        )

    for x in range(cx):
        w = [w_ref[0, c, x] for c in range(3)]
        kappa, mu, atten = kappa_ref[x], mu_ref[x], at_ref[x]
        bb = DT2 * buoy_ref[x]
        bbmu = bb * mu
        live = mask_ref[x]
        base = []
        for c in range(3):
            total = sm_ref[0, 0, c, x] + sm_ref[0, 1, c, x] + sm_ref[0, 2, c, x]
            value = 2.0 * w[c] - v_ref[0, c, x] - bb * total
            base_ref[c, x] = value
            base.append(value)
        bm = [bm_ref[0, l, x] for l in range(3)]
        zsum = bm[0] + bm[1] + bm[2]
        z1 = decay[0] * bm[0] + decay[1] * bm[1] + decay[2] * bm[2]
        zsum_ref[x] = zsum
        z1_ref[x] = z1
        third = jnp.where(
            row == 2,
            roll(z1, 2, 0),
            jnp.where(
                row == 3,
                roll(atten, 3, 0),
                jnp.where(row == 4, roll(atten, -3, 0), jnp.where(row == 5, roll(z1, -2, 0), bbmu)),
            ),
        )
        tiles = [
            (spare(w[0], live, 3), w[1]),
            (w[2], spare(kappa, live, 2)),
            (zsum, third),
            (pair(base[0], base[1]), pair(base[2], bb)),
        ]
        for t, (a, b) in enumerate(tiles):
            b = roll(b, 4, 0)
            y_refs[0][t, x] = jnp.where(keep, a, b)
            y_refs[1][t, x] = jnp.where(keep, b, a)

    for p in range(np_):
        for (name, d), at in X_AT.items():
            x = jnp.where(((i ^ p) & 1) == 0, cx - d, d - 1)
            if name[0] == "w":
                value = w_ref[0, "xyz".index(name[1]), x]
            elif name == "kappa":
                value = kappa_ref[x]
            elif name == "zsum":
                value = zsum_ref[x]
            elif name == "z1":
                value = z1_ref[x]
            elif name == "atten":
                value = at_ref[x]
            elif name == "mask":
                value = mask_ref[x]
            elif name == "bb":
                value = DT2 * buoy_ref[x]
            elif name == "bbmu":
                value = DT2 * buoy_ref[x] * mu_ref[x]
            else:
                value = base_ref[int(name[4]), x]
            x_refs[p][at] = value
        for q in range(2):
            for at, (t, d) in enumerate(D_LIST):
                x = jnp.where(((i ^ p) & 1) == 0, cx - d, d - 1)
                d_refs[2 * p + q][at] = y_refs[q][t, x]


def first_kernel(
    counts, np_, w_ref, kappa_ref, mu_ref, buoy_ref, at_ref, strain_ref, onset_ref, coef_ref, mask_ref, base_ref, zsum_ref,
    z1_ref, *rest,
):
    nx, ny, cx = counts
    y_refs = rest[:2]
    x_refs = rest[2 : 2 + np_]
    d_refs = rest[2 + np_ : 2 + 3 * np_]
    (term_ref, w1_ref, d0_ref, l0_ref, d1_ref, l1_ref, pb_ref, ph_ref) = rest[2 + 3 * np_ : 10 + 3 * np_]
    (side_ref, halo_ref, p0b, p0h, d0b, d0h, w1b, w1h) = rest[10 + 3 * np_ :]
    i, j = lax.axis_index("gx"), lax.axis_index("gy")
    row = row_of()

    n = len(X_LIST)
    low_there, high_there = i > 0, i < nx - 1
    even = (i & 1) == 0

    def from_sides(pick):
        if np_ == 1:
            value = pick(0)
            return value, value
        first, second = pick(0), pick(1)
        return jnp.where(even, second, first), jnp.where(even, first, second)

    for at in range(n):
        low, high = from_sides(lambda p: x_refs[p][at])
        side_ref[at] = jnp.where(low_there, low, 0.0)
        side_ref[n + at] = jnp.where(high_there, high, 0.0)

    there = jnp.where(row < 4, (j < ny - 1).astype(jnp.int32), (j > 0).astype(jnp.int32))
    mine = (row >> 2) ^ (j & 1)
    pick0, pick1 = jnp.where(mine == 0, there, 0), jnp.where(mine == 1, there, 0)
    swap0, swap1 = roll(pick0, 4, 0), roll(pick1, 4, 0)

    def unpack(t, x, r0, r1, ok):
        if ok is not None:
            r0, r1 = jnp.where(ok, r0, 0.0), jnp.where(ok, r1, 0.0)
        a = jnp.where(pick0 == 1, r0, jnp.where(pick1 == 1, r1, 0.0))
        b = roll(jnp.where(swap0 == 1, r0, jnp.where(swap1 == 1, r1, 0.0)), 4, 0)

        def second(f, near, far):
            return jnp.where(row < 4, roll(f, -near, 0), roll(f, far, 0))

        if t == 0:
            put(("wx", x), a)
            put(("wy", x), b)
            if -2 < x < cx + 1:
                put(("mask", x), jnp.where((row == 0) | (row == 7), second(a, 3, 3), 0.0))
        elif t == 1:
            put(("wz", x), a)
            put(("kappa", x), b)
            if -2 < x < cx + 1:
                live = jnp.where((row == 1) | (row == 6), second(b, 2, 2), halo("mask", x))
                put(("mask", x), live)
        elif t == 2:
            put(("zsum", x), a)
            if -2 < x < cx + 1:
                put(("bbmu", x), b)
            if 0 <= x < cx:
                put(("z1", x), second(b, 2, 2))
                put(("atten", x), second(b, 3, 3))
        else:
            put(("base0", x), a)
            put(("base1", x), second(a, 2, 2))
            put(("base2", x), b)
            put(("bb", x), second(b, 2, 2))

    names = ["wx", "wy", "wz", "kappa", "zsum", "bbmu", "z1", "atten", "base0", "base1", "base2", "bb", "mask"]

    def put(key, value):
        halo_ref[names.index(key[0]), 3 + key[1]] = value

    def halo(name, x):
        return halo_ref[names.index(name), 3 + x]

    for x in range(cx):
        for t in range(4):
            unpack(t, x, y_refs[0][t, x], y_refs[1][t, x], None)
    for at, (t, d) in enumerate(D_LIST):
        low0, high0 = from_sides(lambda p: d_refs[2 * p][at])
        low1, high1 = from_sides(lambda p: d_refs[2 * p + 1][at])
        unpack(t, -d, low0, low1, low_there)
        unpack(t, cx - 1 + d, high0, high1, high_there)

    def block(name, x):
        if x < 0:
            return side_ref[X_AT[(name, -x)]]
        if x >= cx:
            return side_ref[n + X_AT[(name, x - cx + 1)]]
        if name[0] == "w":
            return w_ref[0, "xyz".index(name[1]), x]
        if name == "kappa":
            return kappa_ref[x]
        if name == "zsum":
            return zsum_ref[x]
        if name == "z1":
            return z1_ref[x]
        if name == "atten":
            return at_ref[x]
        if name == "mask":
            return mask_ref[x]
        if name == "bb":
            return DT2 * buoy_ref[x]
        if name == "bbmu":
            return DT2 * buoy_ref[x] * mu_ref[x]
        return base_ref[int(name[4]), x]

    def divergence(get_b, get_h, x, with_halo):
        yb, yh = get_b(1, x), get_h(1, x)
        up, down = yplus(yb, yh), yminus(yb, yh)
        z = get_b(2, x)
        db = 0.5 * (get_b(0, x + 1) - get_b(0, x - 1) + (up[0] - down[0]) + (zplus(z) - zminus(z)))
        if not with_halo:
            return db, None
        z = get_h(2, x)
        dh = 0.5 * (get_h(0, x + 1) - get_h(0, x - 1) + (up[1] - down[1]) + (zplus(z) - zminus(z)))
        return db, dh

    def w_b(c, x):
        return block("w" + "xyz"[c], x)

    def w_h(c, x):
        return halo("w" + "xyz"[c], x)

    for x in range(-3, cx + 3):
        inner = -3 < x < cx + 2
        db, dh = divergence(w_b, w_h, x, inner)
        p0b[3 + x] = block("kappa", x) * db - block("zsum", x)
        if -2 < x < cx + 1:
            d0b[1 + x] = db
        if inner:
            p0h[2 + x] = halo("kappa", x) * dh - halo("zsum", x)
            if 0 <= x < cx:
                d0h[x] = dh
                d0_ref[x] = db

    def lap(get_b, get_h, c, x, with_halo):
        b, h = get_b(c, x), get_h(c, x)
        up, down = yplus(b, h), yminus(b, h)
        lb = get_b(c, x + 1) + get_b(c, x - 1) + (up[0] + down[0]) + (zplus(b) + zminus(b)) - 6.0 * b
        if not with_halo:
            return lb, None
        lh = get_h(c, x + 1) + get_h(c, x - 1) + (up[1] + down[1]) + (zplus(h) + zminus(h)) - 6.0 * h
        return lb, lh

    amp = [coef_ref[6 + c] for c in range(3)]
    slow = [coef_ref[9 + c] for c in range(3)]
    phase_b = wave_phase(slow, onset_ref, counts, row)
    phase_h = wave_phase(slow, onset_ref, counts, jnp.where(row < 4, row + TILE[0], row - TILE[0]))

    for x in range(-2, cx + 2):
        pulse_b = pulse_of(-phase_b(x)) * block("mask", x)
        near = -2 < x < cx + 1
        inside = 0 <= x < cx
        bb, bbmu = block("bb", x), block("bbmu", x)
        if near:
            pb, ph = p0b[3 + x], p0h[2 + x]
            up, down = yplus(pb, ph), yminus(pb, ph)
            grad_b = [0.5 * (p0b[4 + x] - p0b[2 + x]), 0.5 * (up[0] - down[0]), 0.5 * (zplus(pb) - zminus(pb))]
            grad_h = [0.5 * (p0h[3 + x] - p0h[1 + x]), 0.5 * (up[1] - down[1]), 0.5 * (zplus(ph) - zminus(ph))]
            pulse_h = pulse_of(-phase_h(x)) * halo("mask", x)
            hbb, hbbmu = halo("bb", x), halo("bbmu", x)
        else:
            grad_b = [0.5 * (p0b[4 + x] - p0b[2 + x])]
        for c in range(3 if near else 1):
            with_halo = inside or (near and c < 2)
            lb, lh = lap(w_b, w_h, c, x, with_halo)
            value = block(f"base{c}", x) + bb * (grad_b[c] + amp[c] * pulse_b) + bbmu * lb
            w1b[c, 2 + x] = value
            if inside:
                l0_ref[c, x] = lb
                w1_ref[c, x] = value
            if with_halo:
                w1h[c, 1 + x] = halo(f"base{c}", x) + hbb * (grad_h[c] + amp[c] * pulse_h) + hbbmu * lh

    def w1_b(c, x):
        return w1b[c, 2 + x]

    def w1_h(c, x):
        return w1h[c, 1 + x]

    gains = coef_ref[3] + coef_ref[4] + coef_ref[5]
    for x in range(-1, cx + 1):
        inside = 0 <= x < cx
        db, dh = divergence(w1_b, w1_h, x, inside)
        kappa = block("kappa", x)
        stress = kappa * db
        pb_ref[1 + x] = stress - (block("z1", x) + gains * (block("atten", x) * kappa * d0b[1 + x]))
        if not inside:
            continue
        hk = halo("kappa", x)
        ph_ref[x] = hk * dh - (halo("z1", x) + gains * (halo("atten", x) * hk * d0h[x]))
        d1_ref[x] = db
        term_ref[0, x] = kappa * d0b[1 + x] * strain_ref[0, 0, 0, x] + stress * strain_ref[0, 1, 0, x]
        total0, total1 = None, None
        for c in range(3):
            lb, _ = lap(w1_b, w1_h, c, x, False)
            l1_ref[c, x] = lb
            part0 = l0_ref[c, x] * strain_ref[0, 0, 1 + c, x]
            part1 = lb * strain_ref[0, 1, 1 + c, x]
            total0 = part0 if total0 is None else total0 + part0
            total1 = part1 if total1 is None else total1 + part1
        mu = mu_ref[x]
        term_ref[1, x] = mu * total0 + mu * total1


def last_kernel(
    counts, w_ref, bm_ref, sm_ref, kappa_ref, mu_ref, buoy_ref, bat_ref, sat_ref, onset_ref, coef_ref, mask_ref, w1_ref, d0_ref, l0_ref, d1_ref, l1_ref, pb_ref, ph_ref, w2_ref, before_ref, bn_ref, sn_ref,
):
    nx, ny, cx = counts
    decay, gain, amp, slow = ([coef_ref[3 * k + l] for l in range(3)] for k in range(4))
    phase = wave_phase(slow, onset_ref, counts, row_of())
    for x in range(cx):
        bulk = bat_ref[x] * kappa_ref[x]
        q0, q1 = bulk * d0_ref[x], bulk * d1_ref[x]
        for l in range(3):
            now = decay[l] * bm_ref[0, l, x] + gain[l] * q0
            bn_ref[0, l, x] = decay[l] * now + gain[l] * q1
        pb = pb_ref[1 + x]
        ph = ph_ref[x]
        up, down = yplus(pb, ph), yminus(pb, ph)
        grad = [
            0.5 * (pb_ref[2 + x] - pb_ref[x]),
            0.5 * (up[0] - down[0]),
            0.5 * (zplus(pb) - zminus(pb)),
        ]
        mu = mu_ref[x]
        shear = sat_ref[x] * mu
        pulse = pulse_of(TIME_STEP - phase(x)) * mask_ref[x]
        bb = DT2 * buoy_ref[x]
        for c in range(3):
            l1 = l1_ref[c, x]
            q0, q1 = shear * l0_ref[c, x], shear * l1
            total = None
            for l in range(3):
                now = decay[l] * sm_ref[0, l, c, x] + gain[l] * q0
                sn_ref[0, l, c, x] = decay[l] * now + gain[l] * q1
                total = now if total is None else total + now
            force = grad[c] + mu * l1 - total + amp[c] * pulse
            w1 = w1_ref[c, x]
            before_ref[0, c, x] = w1
            w2_ref[0, c, x] = 2.0 * w1 - w_ref[0, c, x] + bb * force


def matched(value, mesh_shape, along_x, along_y, p, q):
    nx, ny = mesh_shape
    pairs = []
    for a in range(nx):
        for b in range(ny):
            c, d = a, b
            if along_x:
                c = a + 1 if a % 2 == p else a - 1
            if along_y:
                d = b + 1 if b % 2 == q else b - 1
            if not (0 <= c < nx and 0 <= d < ny):
                c, d = a, b
            pairs.append((a * ny + b, c * ny + d))
    return lax.ppermute(value, ("gx", "gy"), pairs)


def event_sum(value):
    count = lax.axis_size("event")
    if count & (count - 1):
        return lax.psum(value, "event")
    step = 1
    while step < count:
        value = value + lax.ppermute(value, "event", [(e, e ^ step) for e in range(count)])
        step *= 2
    return value


def vmem():
    return pl.BlockSpec(memory_space=pltpu.VMEM)


def smem():
    return pl.BlockSpec(memory_space=pltpu.SMEM)


def body(
    adjoint_now, adjoint_old, bulk_memory, shear_memory, forward_strain, bulk_modulus, shear_modulus, buoyancy,
    bulk_atten, shear_atten, relax_time, mechanism_weight, event_slowness, event_amplitude, event_onset,
    boundary_cells, boundary_count,
):
    nx, ny = lax.axis_size("gx"), lax.axis_size("gy")
    cx = bulk_modulus.shape[0]
    counts = (nx, ny, cx)
    np_ = 1 if nx == 2 else 2
    f32 = jnp.float32

    def field(*lead):
        return jax.ShapeDtypeStruct((*lead, *TILE), f32)

    params = pltpu.CompilerParams(vmem_limit_bytes=24 * 1024 * 1024)
    pack_args = (
        boundary_count, boundary_cells, relax_time, mechanism_weight, event_slowness, event_amplitude,
        buoyancy, shear_modulus, bulk_modulus, bulk_atten, adjoint_now, adjoint_old, bulk_memory, shear_memory,
    )
    packed = pl.pallas_call(
        functools.partial(pack_kernel, counts, np_),
        out_shape=[field(4, cx)] * 2
        + [field(len(X_LIST))] * np_
        + [field(len(D_LIST))] * (2 * np_)
        + [field(cx), field(12), field(3, cx), field(cx), field(cx)],
        in_specs=[
            pl.BlockSpec(memory_space=pltpu.HBM if given.size > 1 else pltpu.SMEM) for given in pack_args
        ],
        out_specs=[vmem()] * (2 + 3 * np_ + 5),
        scratch_shapes=[
            (pltpu.SMEM if k in (1, 2, 3, 4) else pltpu.VMEM)(given.shape, given.dtype)
            for k, given in enumerate(pack_args[1:])
        ]
        + [pltpu.SemaphoreType.DMA((PACK_ARGS - 1,))],
        compiler_params=params,
        name="pack",
    )(
        *(
            pltpu.with_memory_space_constraint(given, pltpu.HBM) if given.size > 1 else given
            for given in pack_args
        )
    )
    shape = (nx, ny)
    ys = [matched(packed[q], shape, False, True, 0, q) for q in range(2)]
    xs = [matched(packed[2 + p], shape, True, False, p, 0) for p in range(np_)]
    ds = [
        matched(packed[2 + np_ + 2 * p + q], shape, True, True, p, q) for p in range(np_) for q in range(2)
    ]
    mask, coef, base, zsum, z1 = packed[2 + 3 * np_ :]

    first = pl.pallas_call(
        functools.partial(first_kernel, counts, np_),
        out_shape=[
            field(2, cx), field(3, cx), field(cx), field(3, cx), field(cx), field(3, cx), field(cx + 2), field(cx),
        ],
        in_specs=[vmem()] * 6 + [smem()] + [vmem()] * (7 + 3 * np_),
        out_specs=[vmem()] * 8,
        scratch_shapes=[
            pltpu.VMEM((2 * len(X_LIST), *TILE), f32),
            pltpu.VMEM((13, cx + 6, *TILE), f32),
            pltpu.VMEM((cx + 6, *TILE), f32),
            pltpu.VMEM((cx + 4, *TILE), f32),
            pltpu.VMEM((cx + 2, *TILE), f32),
            pltpu.VMEM((cx, *TILE), f32),
            pltpu.VMEM((3, cx + 4, *TILE), f32),
            pltpu.VMEM((3, cx + 2, *TILE), f32),
        ],
        compiler_params=params,
        name="first",
    )(
        adjoint_now, bulk_modulus, shear_modulus, buoyancy, bulk_atten, forward_strain, event_onset, coef, mask, base, zsum, z1, *ys, *xs, *ds,
    )
    term, w1, d0, l0, d1, l1, pb, ph = first
    total = event_sum(term)

    w2, before, bulk_next, shear_next = pl.pallas_call(
        functools.partial(last_kernel, counts),
        out_shape=[field(1, 3, cx), field(1, 3, cx), field(1, 3, cx), field(1, 3, 3, cx)],
        in_specs=[vmem()] * 8 + [smem()] + [vmem()] * 9,
        out_specs=[vmem()] * 4,
        compiler_params=params,
        cost_estimate=pl.CostEstimate(flops=3_000_000, bytes_accessed=4_000_000, transcendentals=0),
        name="last",
    )(
        adjoint_now, bulk_memory, shear_memory, bulk_modulus, shear_modulus, buoyancy, bulk_atten, shear_atten,
        event_onset, coef, mask, w1, d0, l0, d1, l1, pb, ph,
    )
    return w2, before, bulk_next, shear_next, total[0], total[1]


def solution(mesh):
    wide = P("event", None, "gx", "gy", None)
    wider = P("event", None, None, "gx", "gy", None)
    grid = P("gx", "gy", None)
    return jax.shard_map(
        body,
        mesh=mesh,
        in_specs=(
            wide, wide, wide, wider, wider, grid, grid, grid, grid, grid, P(), P(), P("event", None),
            P("event", None), P("event"), grid, P("gx", "gy"),
        ),
        out_specs=(wide, wide, wide, wider, grid, grid),
        check_vma=False,
    )
```

```python
import functools

import jax
import jax.numpy as jnp
from jax import lax
from jax.experimental import pallas as pl
from jax.experimental.pallas import tpu as pltpu
from jax.sharding import PartitionSpec as P

TIME_STEP = 0.3
DT2 = TIME_STEP * TIME_STEP
TILE = (8, 128)

X_LIST = (
    [("wx", d) for d in (1, 2, 3, 4)]
    + [("wy", d) for d in (1, 2, 3)]
    + [("wz", d) for d in (1, 2, 3)]
    + [("kappa", d) for d in (1, 2, 3)]
    + [("zsum", d) for d in (1, 2, 3)]
    + [(f"base{c}", d) for c in range(3) for d in (1, 2)]
    + [("bb", d) for d in (1, 2)]
    + [("bbmu", d) for d in (1, 2)]
    + [("z1", 1), ("atten", 1), ("mask", 1), ("mask", 2)]
)
X_AT = {key: at for at, key in enumerate(X_LIST)}
PACK_ARGS, SMALL, KEPT, PARTS = 14, 5, (6, 7, 8, 9, 10), 2
D_LIST = [(t, 1) for t in range(4)] + [(t, 2) for t in range(3)] + [(0, 3)]


def roll(tile, shift, axis):
    return pltpu.roll(tile, shift % TILE[axis], axis)


def row_of():
    return lax.broadcasted_iota(jnp.int32, TILE, 0)


def lane_of():
    return lax.broadcasted_iota(jnp.int32, TILE, 1)


def zplus(f):
    return jnp.where(lane_of() == TILE[1] - 1, 0.0, roll(f, -1, 1))


def zminus(f):
    return jnp.where(lane_of() == 0, 0.0, roll(f, 1, 1))


def yplus(block, halo):
    b, h = roll(block, -1, 0), roll(halo, -1, 0)
    last = row_of() == TILE[0] - 1
    return jnp.where(last, h, b), jnp.where(last, b, h)


def yminus(block, halo):
    b, h = roll(block, 1, 0), roll(halo, 1, 0)
    first = row_of() == 0
    return jnp.where(first, h, b), jnp.where(first, b, h)


def decay_gain(relax_ref, weight_ref):
    decay, gain = [], []
    for l in range(relax_ref.shape[0]):
        d = jnp.exp(-TIME_STEP / jnp.full(TILE, relax_ref[l], jnp.float32))
        decay.append(d)
        gain.append((1.0 - d) * weight_ref[l])
    return decay, gain


def wave_phase(slow, onset_ref, counts, y):
    nx, ny, cx = counts
    i, j = lax.axis_index("gx"), lax.axis_index("gy")
    py = (j * TILE[0] + y).astype(jnp.float32) / float(ny * TILE[0])
    pz = lane_of().astype(jnp.float32) / float(TILE[1])
    common = slow[1] * py + slow[2] * pz + onset_ref[0]

    def at(x):
        px = jnp.full(TILE, i * cx + x, jnp.int32).astype(jnp.float32) / float(nx * cx)
        return slow[0] * px + common

    return at


def pulse_of(tau):
    square = tau * tau
    return (1.0 - 2.0 * square) * jnp.exp(-square)


def pack_kernel(
    counts, np_, *refs,
):
    nx, ny, cx = counts
    count_ref, given, rest = refs[0], refs[1:PACK_ARGS], refs[PACK_ARGS:]
    n = 7 + 3 * np_
    outs, kept, own, sems = rest[:n], rest[n : n + len(KEPT)], rest[n + len(KEPT) : -1], rest[-1]
    held = (*own[:SMALL], *kept, *own[SMALL:])
    pairs = list(zip(given[:SMALL], held[:SMALL]))
    for part in range(PARTS):
        planes = pl.ds(part * (cx // PARTS), cx // PARTS)
        for a, b in zip(given[SMALL:], held[SMALL:]):
            lead = (slice(None),) * (len(a.shape) - 3)
            pairs.append((a.at[(*lead, planes)], b.at[(*lead, planes)]))
    copies = [pltpu.make_async_copy(a, b, sems.at[k]) for k, (a, b) in enumerate(pairs)]
    for copy in copies:
        copy.start()
    (cells_ref, relax_ref, weight_ref, slow_ref, amp_ref, buoy_ref, mu_ref, kappa_ref, at_ref, w_ref, v_ref, bm_ref,
     sm_ref) = held
    y_refs = outs[:2]
    x_refs = outs[2 : 2 + np_]
    d_refs = outs[2 + np_ : 2 + 3 * np_]
    mask_ref, coef_ref, base_ref, zsum_ref, z1_ref = outs[2 + 3 * np_ :]
    i, j = lax.axis_index("gx"), lax.axis_index("gy")
    rows = cx * TILE[0]
    slots = cells_ref.shape[2]
    copies[0].wait()
    cells = cells_ref[0]
    slot = lax.broadcasted_iota(jnp.int32, (1, slots), 1)
    live = slot < count_ref[0, 0]
    row_id = jnp.where(live, cells >> 7, -1)
    lane_id = cells & (TILE[1] - 1)
    wide = lax.broadcasted_iota(jnp.int32, (rows, slots), 0)
    hot_row = jnp.where(wide == row_id, 1.0, 0.0).astype(jnp.bfloat16)
    deep = lax.broadcasted_iota(jnp.int32, (TILE[1], slots), 0)
    hot_lane = jnp.where(deep == lane_id, 1.0, 0.0).astype(jnp.bfloat16)
    mask = lax.dot_general(
        hot_row, hot_lane, (((1,), (1,)), ((), ())), preferred_element_type=jnp.float32
    )
    mask_ref[...] = mask.reshape(cx, TILE[0], TILE[1])

    for copy in copies[1:SMALL]:
        copy.wait()
    decay, gain = decay_gain(relax_ref, weight_ref)
    for l in range(3):
        coef_ref[l] = decay[l]
        coef_ref[3 + l] = gain[l]
        coef_ref[6 + l] = jnp.full(TILE, amp_ref[0, l], jnp.float32)
        coef_ref[9 + l] = jnp.full(TILE, slow_ref[0, l], jnp.float32)
    row = row_of()
    keep = ((row >> 2) ^ (j & 1)) == 1
    two_three = (row == 2) | (row == 3)
    four_five = (row == 4) | (row == 5)

    def pair(first, second):
        return jnp.where(
            two_three, roll(second, 2, 0), jnp.where(four_five, roll(second, -2, 0), first)
        )

    def spare(field, live, shift):
        return jnp.where(
            row == 3, roll(live, shift, 0), jnp.where(row == 4, roll(live, -shift, 0), field)
        )

    size = len(given) - SMALL
    for x in range(cx):
        if x % (cx // PARTS) == 0:
            at = SMALL + x // (cx // PARTS) * size
            for copy in copies[at : at + size]:
                copy.wait()
        w = [w_ref[0, c, x] for c in range(3)]
        kappa, mu, atten = kappa_ref[x], mu_ref[x], at_ref[x]
        bb = DT2 * buoy_ref[x]
        bbmu = bb * mu
        live = mask_ref[x]
        base = []
        for c in range(3):
            total = sm_ref[0, 0, c, x] + sm_ref[0, 1, c, x] + sm_ref[0, 2, c, x]
            value = 2.0 * w[c] - v_ref[0, c, x] - bb * total
            base_ref[c, x] = value
            base.append(value)
        bm = [bm_ref[0, l, x] for l in range(3)]
        zsum = bm[0] + bm[1] + bm[2]
        z1 = decay[0] * bm[0] + decay[1] * bm[1] + decay[2] * bm[2]
        zsum_ref[x] = zsum
        z1_ref[x] = z1
        third = jnp.where(
            row == 2,
            roll(z1, 2, 0),
            jnp.where(
                row == 3,
                roll(atten, 3, 0),
                jnp.where(row == 4, roll(atten, -3, 0), jnp.where(row == 5, roll(z1, -2, 0), bbmu)),
            ),
        )
        tiles = [
            (spare(w[0], live, 3), w[1]),
            (w[2], spare(kappa, live, 2)),
            (zsum, third),
            (pair(base[0], base[1]), pair(base[2], bb)),
        ]
        for t, (a, b) in enumerate(tiles):
            b = roll(b, 4, 0)
            y_refs[0][t, x] = jnp.where(keep, a, b)
            y_refs[1][t, x] = jnp.where(keep, b, a)

    for p in range(np_):
        for (name, d), at in X_AT.items():
            x = jnp.where(((i ^ p) & 1) == 0, cx - d, d - 1)
            if name[0] == "w":
                value = w_ref[0, "xyz".index(name[1]), x]
            elif name == "kappa":
                value = kappa_ref[x]
            elif name == "zsum":
                value = zsum_ref[x]
            elif name == "z1":
                value = z1_ref[x]
            elif name == "atten":
                value = at_ref[x]
            elif name == "mask":
                value = mask_ref[x]
            elif name == "bb":
                value = DT2 * buoy_ref[x]
            elif name == "bbmu":
                value = DT2 * buoy_ref[x] * mu_ref[x]
            else:
                value = base_ref[int(name[4]), x]
            x_refs[p][at] = value
        for q in range(2):
            for at, (t, d) in enumerate(D_LIST):
                x = jnp.where(((i ^ p) & 1) == 0, cx - d, d - 1)
                d_refs[2 * p + q][at] = y_refs[q][t, x]


def first_kernel(
    counts, np_, w_ref, kappa_ref, mu_ref, buoy_ref, at_ref, strain_ref, onset_ref, coef_ref, mask_ref, base_ref, zsum_ref,
    z1_ref, *rest,
):
    nx, ny, cx = counts
    y_refs = rest[:2]
    x_refs = rest[2 : 2 + np_]
    d_refs = rest[2 + np_ : 2 + 3 * np_]
    (term_ref, w1_ref, d0_ref, l0_ref, d1_ref, l1_ref, pb_ref, ph_ref) = rest[2 + 3 * np_ : 10 + 3 * np_]
    (side_ref, halo_ref, p0b, p0h, d0b, d0h, w1b, w1h) = rest[10 + 3 * np_ :]
    i, j = lax.axis_index("gx"), lax.axis_index("gy")
    row = row_of()

    n = len(X_LIST)
    low_there, high_there = i > 0, i < nx - 1
    even = (i & 1) == 0

    def from_sides(pick):
        if np_ == 1:
            value = pick(0)
            return value, value
        first, second = pick(0), pick(1)
        return jnp.where(even, second, first), jnp.where(even, first, second)

    for at in range(n):
        low, high = from_sides(lambda p: x_refs[p][at])
        side_ref[at] = jnp.where(low_there, low, 0.0)
        side_ref[n + at] = jnp.where(high_there, high, 0.0)

    there = jnp.where(row < 4, (j < ny - 1).astype(jnp.int32), (j > 0).astype(jnp.int32))
    mine = (row >> 2) ^ (j & 1)
    pick0, pick1 = jnp.where(mine == 0, there, 0), jnp.where(mine == 1, there, 0)
    swap0, swap1 = roll(pick0, 4, 0), roll(pick1, 4, 0)

    def unpack(t, x, r0, r1, ok):
        if ok is not None:
            r0, r1 = jnp.where(ok, r0, 0.0), jnp.where(ok, r1, 0.0)
        a = jnp.where(pick0 == 1, r0, jnp.where(pick1 == 1, r1, 0.0))
        b = roll(jnp.where(swap0 == 1, r0, jnp.where(swap1 == 1, r1, 0.0)), 4, 0)

        def second(f, near, far):
            return jnp.where(row < 4, roll(f, -near, 0), roll(f, far, 0))

        if t == 0:
            put(("wx", x), a)
            put(("wy", x), b)
            if -2 < x < cx + 1:
                put(("mask", x), jnp.where((row == 0) | (row == 7), second(a, 3, 3), 0.0))
        elif t == 1:
            put(("wz", x), a)
            put(("kappa", x), b)
            if -2 < x < cx + 1:
                live = jnp.where((row == 1) | (row == 6), second(b, 2, 2), halo("mask", x))
                put(("mask", x), live)
        elif t == 2:
            put(("zsum", x), a)
            if -2 < x < cx + 1:
                put(("bbmu", x), b)
            if 0 <= x < cx:
                put(("z1", x), second(b, 2, 2))
                put(("atten", x), second(b, 3, 3))
        else:
            put(("base0", x), a)
            put(("base1", x), second(a, 2, 2))
            put(("base2", x), b)
            put(("bb", x), second(b, 2, 2))

    names = ["wx", "wy", "wz", "kappa", "zsum", "bbmu", "z1", "atten", "base0", "base1", "base2", "bb", "mask"]

    def put(key, value):
        halo_ref[names.index(key[0]), 3 + key[1]] = value

    def halo(name, x):
        return halo_ref[names.index(name), 3 + x]

    for x in range(cx):
        for t in range(4):
            unpack(t, x, y_refs[0][t, x], y_refs[1][t, x], None)
    for at, (t, d) in enumerate(D_LIST):
        low0, high0 = from_sides(lambda p: d_refs[2 * p][at])
        low1, high1 = from_sides(lambda p: d_refs[2 * p + 1][at])
        unpack(t, -d, low0, low1, low_there)
        unpack(t, cx - 1 + d, high0, high1, high_there)

    def block(name, x):
        if x < 0:
            return side_ref[X_AT[(name, -x)]]
        if x >= cx:
            return side_ref[n + X_AT[(name, x - cx + 1)]]
        if name[0] == "w":
            return w_ref[0, "xyz".index(name[1]), x]
        if name == "kappa":
            return kappa_ref[x]
        if name == "zsum":
            return zsum_ref[x]
        if name == "z1":
            return z1_ref[x]
        if name == "atten":
            return at_ref[x]
        if name == "mask":
            return mask_ref[x]
        if name == "bb":
            return DT2 * buoy_ref[x]
        if name == "bbmu":
            return DT2 * buoy_ref[x] * mu_ref[x]
        return base_ref[int(name[4]), x]

    def divergence(get_b, get_h, x, with_halo):
        yb, yh = get_b(1, x), get_h(1, x)
        up, down = yplus(yb, yh), yminus(yb, yh)
        z = get_b(2, x)
        db = 0.5 * (get_b(0, x + 1) - get_b(0, x - 1) + (up[0] - down[0]) + (zplus(z) - zminus(z)))
        if not with_halo:
            return db, None
        z = get_h(2, x)
        dh = 0.5 * (get_h(0, x + 1) - get_h(0, x - 1) + (up[1] - down[1]) + (zplus(z) - zminus(z)))
        return db, dh

    def w_b(c, x):
        return block("w" + "xyz"[c], x)

    def w_h(c, x):
        return halo("w" + "xyz"[c], x)

    for x in range(-3, cx + 3):
        inner = -3 < x < cx + 2
        db, dh = divergence(w_b, w_h, x, inner)
        p0b[3 + x] = block("kappa", x) * db - block("zsum", x)
        if -2 < x < cx + 1:
            d0b[1 + x] = db
        if inner:
            p0h[2 + x] = halo("kappa", x) * dh - halo("zsum", x)
            if 0 <= x < cx:
                d0h[x] = dh
                d0_ref[x] = db

    def lap(get_b, get_h, c, x, with_halo):
        b, h = get_b(c, x), get_h(c, x)
        up, down = yplus(b, h), yminus(b, h)
        lb = get_b(c, x + 1) + get_b(c, x - 1) + (up[0] + down[0]) + (zplus(b) + zminus(b)) - 6.0 * b
        if not with_halo:
            return lb, None
        lh = get_h(c, x + 1) + get_h(c, x - 1) + (up[1] + down[1]) + (zplus(h) + zminus(h)) - 6.0 * h
        return lb, lh

    amp = [coef_ref[6 + c] for c in range(3)]
    slow = [coef_ref[9 + c] for c in range(3)]
    phase_b = wave_phase(slow, onset_ref, counts, row)
    phase_h = wave_phase(slow, onset_ref, counts, jnp.where(row < 4, row + TILE[0], row - TILE[0]))

    for x in range(-2, cx + 2):
        pulse_b = pulse_of(-phase_b(x)) * block("mask", x)
        near = -2 < x < cx + 1
        inside = 0 <= x < cx
        bb, bbmu = block("bb", x), block("bbmu", x)
        if near:
            pb, ph = p0b[3 + x], p0h[2 + x]
            up, down = yplus(pb, ph), yminus(pb, ph)
            grad_b = [0.5 * (p0b[4 + x] - p0b[2 + x]), 0.5 * (up[0] - down[0]), 0.5 * (zplus(pb) - zminus(pb))]
            grad_h = [0.5 * (p0h[3 + x] - p0h[1 + x]), 0.5 * (up[1] - down[1]), 0.5 * (zplus(ph) - zminus(ph))]
            pulse_h = pulse_of(-phase_h(x)) * halo("mask", x)
            hbb, hbbmu = halo("bb", x), halo("bbmu", x)
        else:
            grad_b = [0.5 * (p0b[4 + x] - p0b[2 + x])]
        for c in range(3 if near else 1):
            with_halo = inside or (near and c < 2)
            lb, lh = lap(w_b, w_h, c, x, with_halo)
            value = block(f"base{c}", x) + bb * (grad_b[c] + amp[c] * pulse_b) + bbmu * lb
            w1b[c, 2 + x] = value
            if inside:
                l0_ref[c, x] = lb
                w1_ref[c, x] = value
            if with_halo:
                w1h[c, 1 + x] = halo(f"base{c}", x) + hbb * (grad_h[c] + amp[c] * pulse_h) + hbbmu * lh

    def w1_b(c, x):
        return w1b[c, 2 + x]

    def w1_h(c, x):
        return w1h[c, 1 + x]

    gains = coef_ref[3] + coef_ref[4] + coef_ref[5]
    for x in range(-1, cx + 1):
        inside = 0 <= x < cx
        db, dh = divergence(w1_b, w1_h, x, inside)
        kappa = block("kappa", x)
        stress = kappa * db
        pb_ref[1 + x] = stress - (block("z1", x) + gains * (block("atten", x) * kappa * d0b[1 + x]))
        if not inside:
            continue
        hk = halo("kappa", x)
        ph_ref[x] = hk * dh - (halo("z1", x) + gains * (halo("atten", x) * hk * d0h[x]))
        d1_ref[x] = db
        term_ref[0, x] = kappa * d0b[1 + x] * strain_ref[0, 0, 0, x] + stress * strain_ref[0, 1, 0, x]
        total0, total1 = None, None
        for c in range(3):
            lb, _ = lap(w1_b, w1_h, c, x, False)
            l1_ref[c, x] = lb
            part0 = l0_ref[c, x] * strain_ref[0, 0, 1 + c, x]
            part1 = lb * strain_ref[0, 1, 1 + c, x]
            total0 = part0 if total0 is None else total0 + part0
            total1 = part1 if total1 is None else total1 + part1
        mu = mu_ref[x]
        term_ref[1, x] = mu * total0 + mu * total1


def last_kernel(
    counts, w_ref, bm_ref, sm_ref, kappa_ref, mu_ref, buoy_ref, bat_ref, sat_ref, onset_ref, coef_ref, mask_ref, w1_ref, d0_ref, l0_ref, d1_ref, l1_ref, pb_ref, ph_ref, w2_ref, before_ref, bn_ref, sn_ref,
):
    nx, ny, cx = counts
    decay, gain, amp, slow = ([coef_ref[3 * k + l] for l in range(3)] for k in range(4))
    phase = wave_phase(slow, onset_ref, counts, row_of())
    for x in range(cx):
        bulk = bat_ref[x] * kappa_ref[x]
        q0, q1 = bulk * d0_ref[x], bulk * d1_ref[x]
        for l in range(3):
            now = decay[l] * bm_ref[0, l, x] + gain[l] * q0
            bn_ref[0, l, x] = decay[l] * now + gain[l] * q1
        pb = pb_ref[1 + x]
        ph = ph_ref[x]
        up, down = yplus(pb, ph), yminus(pb, ph)
        grad = [
            0.5 * (pb_ref[2 + x] - pb_ref[x]),
            0.5 * (up[0] - down[0]),
            0.5 * (zplus(pb) - zminus(pb)),
        ]
        mu = mu_ref[x]
        shear = sat_ref[x] * mu
        pulse = pulse_of(TIME_STEP - phase(x)) * mask_ref[x]
        bb = DT2 * buoy_ref[x]
        for c in range(3):
            l1 = l1_ref[c, x]
            q0, q1 = shear * l0_ref[c, x], shear * l1
            total = None
            for l in range(3):
                now = decay[l] * sm_ref[0, l, c, x] + gain[l] * q0
                sn_ref[0, l, c, x] = decay[l] * now + gain[l] * q1
                total = now if total is None else total + now
            force = grad[c] + mu * l1 - total + amp[c] * pulse
            w1 = w1_ref[c, x]
            before_ref[0, c, x] = w1
            w2_ref[0, c, x] = 2.0 * w1 - w_ref[0, c, x] + bb * force


def matched(value, mesh_shape, along_x, along_y, p, q):
    nx, ny = mesh_shape
    pairs = []
    for a in range(nx):
        for b in range(ny):
            c, d = a, b
            if along_x:
                c = a + 1 if a % 2 == p else a - 1
            if along_y:
                d = b + 1 if b % 2 == q else b - 1
            if not (0 <= c < nx and 0 <= d < ny):
                c, d = a, b
            pairs.append((a * ny + b, c * ny + d))
    return lax.ppermute(value, ("gx", "gy"), pairs)


def event_sum(value):
    count = lax.axis_size("event")
    if count & (count - 1):
        return lax.psum(value, "event")
    step = 1
    while step < count:
        value = value + lax.ppermute(value, "event", [(e, e ^ step) for e in range(count)])
        step *= 2
    return value


def vmem():
    return pl.BlockSpec(memory_space=pltpu.VMEM)


def smem():
    return pl.BlockSpec(memory_space=pltpu.SMEM)


def body(
    adjoint_now, adjoint_old, bulk_memory, shear_memory, forward_strain, bulk_modulus, shear_modulus, buoyancy,
    bulk_atten, shear_atten, relax_time, mechanism_weight, event_slowness, event_amplitude, event_onset,
    boundary_cells, boundary_count,
):
    nx, ny = lax.axis_size("gx"), lax.axis_size("gy")
    cx = bulk_modulus.shape[0]
    counts = (nx, ny, cx)
    np_ = 1 if nx == 2 else 2
    f32 = jnp.float32

    def field(*lead):
        return jax.ShapeDtypeStruct((*lead, *TILE), f32)

    params = pltpu.CompilerParams(vmem_limit_bytes=24 * 1024 * 1024)
    pack_args = (
        boundary_count, boundary_cells, relax_time, mechanism_weight, event_slowness, event_amplitude,
        buoyancy, shear_modulus, bulk_modulus, bulk_atten, adjoint_now, adjoint_old, bulk_memory, shear_memory,
    )
    packed = pl.pallas_call(
        functools.partial(pack_kernel, counts, np_),
        out_shape=[field(4, cx)] * 2
        + [field(len(X_LIST))] * np_
        + [field(len(D_LIST))] * (2 * np_)
        + [field(cx), field(12), field(3, cx), field(cx), field(cx)]
        + [jax.ShapeDtypeStruct(pack_args[k].shape, f32) for k in KEPT],
        in_specs=[
            pl.BlockSpec(memory_space=pltpu.HBM if given.size > 1 else pltpu.SMEM) for given in pack_args
        ],
        out_specs=[vmem()] * (2 + 3 * np_ + 5 + len(KEPT)),
        scratch_shapes=[
            (pltpu.SMEM if k in (1, 2, 3, 4) else pltpu.VMEM)(given.shape, given.dtype)
            for k, given in enumerate(pack_args[1:])
            if k + 1 not in KEPT
        ]
        + [pltpu.SemaphoreType.DMA((SMALL + PARTS * (PACK_ARGS - 1 - SMALL),))],
        compiler_params=params,
        name="pack",
    )(
        *(
            pltpu.with_memory_space_constraint(given, pltpu.HBM) if given.size > 1 else given
            for given in pack_args
        )
    )
    shape = (nx, ny)
    ys = [matched(packed[q], shape, False, True, 0, q) for q in range(2)]
    xs = [matched(packed[2 + p], shape, True, False, p, 0) for p in range(np_)]
    ds = [
        matched(packed[2 + np_ + 2 * p + q], shape, True, True, p, q) for p in range(np_) for q in range(2)
    ]
    mask, coef, base, zsum, z1, inverse, shear, bulk, atten, wave = packed[2 + 3 * np_ :]

    first = pl.pallas_call(
        functools.partial(first_kernel, counts, np_),
        out_shape=[
            field(2, cx), field(3, cx), field(cx), field(3, cx), field(cx), field(3, cx), field(cx + 2), field(cx),
        ],
        in_specs=[vmem()] * 6 + [smem()] + [vmem()] * (7 + 3 * np_),
        out_specs=[vmem()] * 8,
        scratch_shapes=[
            pltpu.VMEM((2 * len(X_LIST), *TILE), f32),
            pltpu.VMEM((13, cx + 6, *TILE), f32),
            pltpu.VMEM((cx + 6, *TILE), f32),
            pltpu.VMEM((cx + 4, *TILE), f32),
            pltpu.VMEM((cx + 2, *TILE), f32),
            pltpu.VMEM((cx, *TILE), f32),
            pltpu.VMEM((3, cx + 4, *TILE), f32),
            pltpu.VMEM((3, cx + 2, *TILE), f32),
        ],
        compiler_params=params,
        name="first",
    )(
        wave, bulk, shear, inverse, atten, forward_strain, event_onset, coef, mask, base, zsum, z1, *ys, *xs, *ds,
    )
    term, w1, d0, l0, d1, l1, pb, ph = first
    total = event_sum(term)

    w2, before, bulk_next, shear_next = pl.pallas_call(
        functools.partial(last_kernel, counts),
        out_shape=[field(1, 3, cx), field(1, 3, cx), field(1, 3, cx), field(1, 3, 3, cx)],
        in_specs=[vmem()] * 8 + [smem()] + [vmem()] * 9,
        out_specs=[vmem()] * 4,
        compiler_params=params,
        cost_estimate=pl.CostEstimate(flops=3_000_000, bytes_accessed=4_000_000, transcendentals=0),
        name="last",
    )(
        wave, bulk_memory, shear_memory, bulk, shear, inverse, atten, shear_atten,
        event_onset, coef, mask, w1, d0, l0, d1, l1, pb, ph,
    )
    return w2, before, bulk_next, shear_next, total[0], total[1]


def solution(mesh):
    wide = P("event", None, "gx", "gy", None)
    wider = P("event", None, None, "gx", "gy", None)
    grid = P("gx", "gy", None)
    return jax.shard_map(
        body,
        mesh=mesh,
        in_specs=(
            wide, wide, wide, wider, wider, grid, grid, grid, grid, grid, P(), P(), P("event", None),
            P("event", None), P("event"), grid, P("gx", "gy"),
        ),
        out_specs=(wide, wide, wide, wider, grid, grid),
        check_vma=False,
    )
```

```python
import functools

import jax
import jax.numpy as jnp
from jax import lax
from jax.experimental import pallas as pl
from jax.experimental.pallas import tpu as pltpu
from jax.sharding import PartitionSpec as P

TIME_STEP = 0.3
DT2 = TIME_STEP * TIME_STEP
TILE = (8, 128)

X_LIST = (
    [("wx", d) for d in (1, 2, 3, 4)]
    + [("wy", d) for d in (1, 2, 3)]
    + [("wz", d) for d in (1, 2, 3)]
    + [("kappa", d) for d in (1, 2, 3)]
    + [("zsum", d) for d in (1, 2, 3)]
    + [(f"base{c}", d) for c in range(3) for d in (1, 2)]
    + [("bb", d) for d in (1, 2)]
    + [("bbmu", d) for d in (1, 2)]
    + [("z1", 1), ("atten", 1), ("mask", 1), ("mask", 2)]
)
X_AT = {key: at for at, key in enumerate(X_LIST)}
PACK_ARGS, SMALL, KEPT, PARTS = 14, 5, (6, 7, 8, 9, 10), 2
D_LIST = [(t, 1) for t in range(4)] + [(t, 2) for t in range(3)] + [(0, 3)]


def roll(tile, shift, axis):
    return pltpu.roll(tile, shift % TILE[axis], axis)


def row_of():
    return lax.broadcasted_iota(jnp.int32, TILE, 0)


def lane_of():
    return lax.broadcasted_iota(jnp.int32, TILE, 1)


def zplus(f):
    return jnp.where(lane_of() == TILE[1] - 1, 0.0, roll(f, -1, 1))


def zminus(f):
    return jnp.where(lane_of() == 0, 0.0, roll(f, 1, 1))


def yplus(block, halo):
    b, h = roll(block, -1, 0), roll(halo, -1, 0)
    last = row_of() == TILE[0] - 1
    return jnp.where(last, h, b), jnp.where(last, b, h)


def yminus(block, halo):
    b, h = roll(block, 1, 0), roll(halo, 1, 0)
    first = row_of() == 0
    return jnp.where(first, h, b), jnp.where(first, b, h)


def decay_gain(relax_ref, weight_ref):
    decay, gain = [], []
    for l in range(relax_ref.shape[0]):
        d = jnp.exp(-TIME_STEP / jnp.full(TILE, relax_ref[l], jnp.float32))
        decay.append(d)
        gain.append((1.0 - d) * weight_ref[l])
    return decay, gain


def wave_phase(slow, onset_ref, counts, y):
    nx, ny, cx = counts
    i, j = lax.axis_index("gx"), lax.axis_index("gy")
    py = (j * TILE[0] + y).astype(jnp.float32) / float(ny * TILE[0])
    pz = lane_of().astype(jnp.float32) / float(TILE[1])
    common = slow[1] * py + slow[2] * pz + onset_ref[0]

    def at(x):
        px = jnp.full(TILE, i * cx + x, jnp.int32).astype(jnp.float32) / float(nx * cx)
        return slow[0] * px + common

    return at


def pulse_of(tau):
    square = tau * tau
    return (1.0 - 2.0 * square) * jnp.exp(-square)


def pack_kernel(
    counts, np_, *refs,
):
    nx, ny, cx = counts
    count_ref, given, rest = refs[0], refs[1:PACK_ARGS], refs[PACK_ARGS:]
    n = 7 + 3 * np_
    outs, kept, own, sems = rest[:n], rest[n : n + len(KEPT)], rest[n + len(KEPT) : -1], rest[-1]
    held = (*own[:SMALL], *kept, *own[SMALL:])
    pairs = list(zip(given[:SMALL], held[:SMALL]))
    for part in range(PARTS):
        planes = pl.ds(part * (cx // PARTS), cx // PARTS)
        for a, b in zip(given[SMALL:], held[SMALL:]):
            lead = (slice(None),) * (len(a.shape) - 3)
            pairs.append((a.at[(*lead, planes)], b.at[(*lead, planes)]))
    copies = [pltpu.make_async_copy(a, b, sems.at[k]) for k, (a, b) in enumerate(pairs)]
    for copy in copies:
        copy.start()
    (cells_ref, relax_ref, weight_ref, slow_ref, amp_ref, buoy_ref, mu_ref, kappa_ref, at_ref, w_ref, v_ref, bm_ref,
     sm_ref) = held
    y_refs = outs[:2]
    x_refs = outs[2 : 2 + np_]
    d_refs = outs[2 + np_ : 2 + 3 * np_]
    mask_ref, coef_ref, base_ref, zsum_ref, z1_ref = outs[2 + 3 * np_ :]
    i, j = lax.axis_index("gx"), lax.axis_index("gy")
    rows = cx * TILE[0]
    slots = cells_ref.shape[2]
    copies[0].wait()
    cells = cells_ref[0]
    slot = lax.broadcasted_iota(jnp.int32, (1, slots), 1)
    live = slot < count_ref[0, 0]
    row_id = jnp.where(live, cells >> 7, -1)
    lane_id = cells & (TILE[1] - 1)
    wide = lax.broadcasted_iota(jnp.int32, (rows, slots), 0)
    hot_row = jnp.where(wide == row_id, 1.0, 0.0).astype(jnp.bfloat16)
    deep = lax.broadcasted_iota(jnp.int32, (TILE[1], slots), 0)
    hot_lane = jnp.where(deep == lane_id, 1.0, 0.0).astype(jnp.bfloat16)
    mask = lax.dot_general(
        hot_row, hot_lane, (((1,), (1,)), ((), ())), preferred_element_type=jnp.float32
    )
    mask_ref[...] = mask.reshape(cx, TILE[0], TILE[1])

    for copy in copies[1:SMALL]:
        copy.wait()
    decay, gain = decay_gain(relax_ref, weight_ref)
    for l in range(3):
        coef_ref[l] = decay[l]
        coef_ref[3 + l] = gain[l]
        coef_ref[6 + l] = jnp.full(TILE, amp_ref[0, l], jnp.float32)
        coef_ref[9 + l] = jnp.full(TILE, slow_ref[0, l], jnp.float32)
    row = row_of()
    keep = ((row >> 2) ^ (j & 1)) == 1
    two_three = (row == 2) | (row == 3)
    four_five = (row == 4) | (row == 5)

    def pair(first, second):
        return jnp.where(
            two_three, roll(second, 2, 0), jnp.where(four_five, roll(second, -2, 0), first)
        )

    def spare(field, live, shift):
        return jnp.where(
            row == 3, roll(live, shift, 0), jnp.where(row == 4, roll(live, -shift, 0), field)
        )

    size = len(given) - SMALL
    for x in range(cx):
        if x % (cx // PARTS) == 0:
            at = SMALL + x // (cx // PARTS) * size
            for copy in copies[at : at + size]:
                copy.wait()
        w = [w_ref[0, c, x] for c in range(3)]
        kappa, mu, atten = kappa_ref[x], mu_ref[x], at_ref[x]
        bb = DT2 * buoy_ref[x]
        bbmu = bb * mu
        live = mask_ref[x]
        base = []
        for c in range(3):
            total = sm_ref[0, 0, c, x] + sm_ref[0, 1, c, x] + sm_ref[0, 2, c, x]
            value = 2.0 * w[c] - v_ref[0, c, x] - bb * total
            base_ref[c, x] = value
            base.append(value)
        bm = [bm_ref[0, l, x] for l in range(3)]
        zsum = bm[0] + bm[1] + bm[2]
        z1 = decay[0] * bm[0] + decay[1] * bm[1] + decay[2] * bm[2]
        zsum_ref[x] = zsum
        z1_ref[x] = z1
        third = jnp.where(
            row == 2,
            roll(z1, 2, 0),
            jnp.where(
                row == 3,
                roll(atten, 3, 0),
                jnp.where(row == 4, roll(atten, -3, 0), jnp.where(row == 5, roll(z1, -2, 0), bbmu)),
            ),
        )
        tiles = [
            (spare(w[0], live, 3), w[1]),
            (w[2], spare(kappa, live, 2)),
            (zsum, third),
            (pair(base[0], base[1]), pair(base[2], bb)),
        ]
        for t, (a, b) in enumerate(tiles):
            b = roll(b, 4, 0)
            y_refs[0][t, x] = jnp.where(keep, a, b)
            y_refs[1][t, x] = jnp.where(keep, b, a)

    for p in range(np_):
        for (name, d), at in X_AT.items():
            x = jnp.where(((i ^ p) & 1) == 0, cx - d, d - 1)
            if name[0] == "w":
                value = w_ref[0, "xyz".index(name[1]), x]
            elif name == "kappa":
                value = kappa_ref[x]
            elif name == "zsum":
                value = zsum_ref[x]
            elif name == "z1":
                value = z1_ref[x]
            elif name == "atten":
                value = at_ref[x]
            elif name == "mask":
                value = mask_ref[x]
            elif name == "bb":
                value = DT2 * buoy_ref[x]
            elif name == "bbmu":
                value = DT2 * buoy_ref[x] * mu_ref[x]
            else:
                value = base_ref[int(name[4]), x]
            x_refs[p][at] = value
        for q in range(2):
            for at, (t, d) in enumerate(D_LIST):
                x = jnp.where(((i ^ p) & 1) == 0, cx - d, d - 1)
                d_refs[2 * p + q][at] = y_refs[q][t, x]


def first_kernel(
    counts, np_, w_ref, kappa_ref, mu_ref, buoy_ref, at_ref, strain_ref, onset_ref, coef_ref, mask_ref, base_ref, zsum_ref,
    z1_ref, *rest,
):
    nx, ny, cx = counts
    y_refs = rest[:2]
    x_refs = rest[2 : 2 + np_]
    d_refs = rest[2 + np_ : 2 + 3 * np_]
    (term_ref, w1_ref, d0_ref, l0_ref, d1_ref, l1_ref, pb_ref, ph_ref) = rest[2 + 3 * np_ : 10 + 3 * np_]
    (side_ref, halo_ref, p0b, p0h, d0b, d0h, w1b, w1h) = rest[10 + 3 * np_ :]
    i, j = lax.axis_index("gx"), lax.axis_index("gy")
    row = row_of()

    n = len(X_LIST)
    low_there, high_there = i > 0, i < nx - 1
    even = (i & 1) == 0

    def from_sides(pick):
        if np_ == 1:
            value = pick(0)
            return value, value
        first, second = pick(0), pick(1)
        return jnp.where(even, second, first), jnp.where(even, first, second)

    for at in range(n):
        low, high = from_sides(lambda p: x_refs[p][at])
        side_ref[at] = jnp.where(low_there, low, 0.0)
        side_ref[n + at] = jnp.where(high_there, high, 0.0)

    there = jnp.where(row < 4, (j < ny - 1).astype(jnp.int32), (j > 0).astype(jnp.int32))
    mine = (row >> 2) ^ (j & 1)
    pick0, pick1 = jnp.where(mine == 0, there, 0), jnp.where(mine == 1, there, 0)
    swap0, swap1 = roll(pick0, 4, 0), roll(pick1, 4, 0)

    def unpack(t, x, r0, r1, ok):
        if ok is not None:
            r0, r1 = jnp.where(ok, r0, 0.0), jnp.where(ok, r1, 0.0)
        a = jnp.where(pick0 == 1, r0, jnp.where(pick1 == 1, r1, 0.0))
        b = roll(jnp.where(swap0 == 1, r0, jnp.where(swap1 == 1, r1, 0.0)), 4, 0)

        def second(f, near, far):
            return jnp.where(row < 4, roll(f, -near, 0), roll(f, far, 0))

        if t == 0:
            put(("wx", x), a)
            put(("wy", x), b)
            if -2 < x < cx + 1:
                put(("mask", x), jnp.where((row == 0) | (row == 7), second(a, 3, 3), 0.0))
        elif t == 1:
            put(("wz", x), a)
            put(("kappa", x), b)
            if -2 < x < cx + 1:
                live = jnp.where((row == 1) | (row == 6), second(b, 2, 2), halo("mask", x))
                put(("mask", x), live)
        elif t == 2:
            put(("zsum", x), a)
            if -2 < x < cx + 1:
                put(("bbmu", x), b)
            if 0 <= x < cx:
                put(("z1", x), second(b, 2, 2))
                put(("atten", x), second(b, 3, 3))
        else:
            put(("base0", x), a)
            put(("base1", x), second(a, 2, 2))
            put(("base2", x), b)
            put(("bb", x), second(b, 2, 2))

    names = ["wx", "wy", "wz", "kappa", "zsum", "bbmu", "z1", "atten", "base0", "base1", "base2", "bb", "mask"]

    def put(key, value):
        halo_ref[names.index(key[0]), 3 + key[1]] = value

    def halo(name, x):
        return halo_ref[names.index(name), 3 + x]

    for x in range(cx):
        for t in range(4):
            unpack(t, x, y_refs[0][t, x], y_refs[1][t, x], None)
    for at, (t, d) in enumerate(D_LIST):
        low0, high0 = from_sides(lambda p: d_refs[2 * p][at])
        low1, high1 = from_sides(lambda p: d_refs[2 * p + 1][at])
        unpack(t, -d, low0, low1, low_there)
        unpack(t, cx - 1 + d, high0, high1, high_there)

    def block(name, x):
        if x < 0:
            return side_ref[X_AT[(name, -x)]]
        if x >= cx:
            return side_ref[n + X_AT[(name, x - cx + 1)]]
        if name[0] == "w":
            return w_ref[0, "xyz".index(name[1]), x]
        if name == "kappa":
            return kappa_ref[x]
        if name == "zsum":
            return zsum_ref[x]
        if name == "z1":
            return z1_ref[x]
        if name == "atten":
            return at_ref[x]
        if name == "mask":
            return mask_ref[x]
        if name == "bb":
            return DT2 * buoy_ref[x]
        if name == "bbmu":
            return DT2 * buoy_ref[x] * mu_ref[x]
        return base_ref[int(name[4]), x]

    def divergence(get_b, get_h, x, with_halo):
        yb, yh = get_b(1, x), get_h(1, x)
        up, down = yplus(yb, yh), yminus(yb, yh)
        z = get_b(2, x)
        db = 0.5 * (get_b(0, x + 1) - get_b(0, x - 1) + (up[0] - down[0]) + (zplus(z) - zminus(z)))
        if not with_halo:
            return db, None
        z = get_h(2, x)
        dh = 0.5 * (get_h(0, x + 1) - get_h(0, x - 1) + (up[1] - down[1]) + (zplus(z) - zminus(z)))
        return db, dh

    def w_b(c, x):
        return block("w" + "xyz"[c], x)

    def w_h(c, x):
        return halo("w" + "xyz"[c], x)

    for x in range(-3, cx + 3):
        inner = -3 < x < cx + 2
        db, dh = divergence(w_b, w_h, x, inner)
        p0b[3 + x] = block("kappa", x) * db - block("zsum", x)
        if -2 < x < cx + 1:
            d0b[1 + x] = db
        if inner:
            p0h[2 + x] = halo("kappa", x) * dh - halo("zsum", x)
            if 0 <= x < cx:
                d0h[x] = dh
                d0_ref[x] = db

    def lap(get_b, get_h, c, x, with_halo):
        b, h = get_b(c, x), get_h(c, x)
        up, down = yplus(b, h), yminus(b, h)
        lb = get_b(c, x + 1) + get_b(c, x - 1) + (up[0] + down[0]) + (zplus(b) + zminus(b)) - 6.0 * b
        if not with_halo:
            return lb, None
        lh = get_h(c, x + 1) + get_h(c, x - 1) + (up[1] + down[1]) + (zplus(h) + zminus(h)) - 6.0 * h
        return lb, lh

    amp = [coef_ref[6 + c] for c in range(3)]
    slow = [coef_ref[9 + c] for c in range(3)]
    phase_b = wave_phase(slow, onset_ref, counts, row)
    phase_h = wave_phase(slow, onset_ref, counts, jnp.where(row < 4, row + TILE[0], row - TILE[0]))

    for x in range(-2, cx + 2):
        pulse_b = pulse_of(-phase_b(x)) * block("mask", x)
        near = -2 < x < cx + 1
        inside = 0 <= x < cx
        bb, bbmu = block("bb", x), block("bbmu", x)
        if near:
            pb, ph = p0b[3 + x], p0h[2 + x]
            up, down = yplus(pb, ph), yminus(pb, ph)
            grad_b = [0.5 * (p0b[4 + x] - p0b[2 + x]), 0.5 * (up[0] - down[0]), 0.5 * (zplus(pb) - zminus(pb))]
            grad_h = [0.5 * (p0h[3 + x] - p0h[1 + x]), 0.5 * (up[1] - down[1]), 0.5 * (zplus(ph) - zminus(ph))]
            pulse_h = pulse_of(-phase_h(x)) * halo("mask", x)
            hbb, hbbmu = halo("bb", x), halo("bbmu", x)
        else:
            grad_b = [0.5 * (p0b[4 + x] - p0b[2 + x])]
        for c in range(3 if near else 1):
            with_halo = inside or (near and c < 2)
            lb, lh = lap(w_b, w_h, c, x, with_halo)
            value = block(f"base{c}", x) + bb * (grad_b[c] + amp[c] * pulse_b) + bbmu * lb
            w1b[c, 2 + x] = value
            if inside:
                l0_ref[c, x] = lb
                w1_ref[c, x] = value
            if with_halo:
                w1h[c, 1 + x] = halo(f"base{c}", x) + hbb * (grad_h[c] + amp[c] * pulse_h) + hbbmu * lh

    def w1_b(c, x):
        return w1b[c, 2 + x]

    def w1_h(c, x):
        return w1h[c, 1 + x]

    gains = coef_ref[3] + coef_ref[4] + coef_ref[5]
    for x in range(-1, cx + 1):
        inside = 0 <= x < cx
        db, dh = divergence(w1_b, w1_h, x, inside)
        kappa = block("kappa", x)
        stress = kappa * db
        pb_ref[1 + x] = stress - (block("z1", x) + gains * (block("atten", x) * kappa * d0b[1 + x]))
        if not inside:
            continue
        hk = halo("kappa", x)
        ph_ref[x] = hk * dh - (halo("z1", x) + gains * (halo("atten", x) * hk * d0h[x]))
        d1_ref[x] = db
        term_ref[0, x] = kappa * d0b[1 + x] * strain_ref[0, 0, 0, x] + stress * strain_ref[0, 1, 0, x]
        total0, total1 = None, None
        for c in range(3):
            lb, _ = lap(w1_b, w1_h, c, x, False)
            l1_ref[c, x] = lb
            part0 = l0_ref[c, x] * strain_ref[0, 0, 1 + c, x]
            part1 = lb * strain_ref[0, 1, 1 + c, x]
            total0 = part0 if total0 is None else total0 + part0
            total1 = part1 if total1 is None else total1 + part1
        mu = mu_ref[x]
        term_ref[1, x] = mu * total0 + mu * total1


def last_kernel(
    counts, w_ref, bm_ref, sm_ref, kappa_ref, mu_ref, buoy_ref, bat_ref, sat_ref, onset_ref, coef_ref, mask_ref, w1_ref, d0_ref, l0_ref, d1_ref, l1_ref, pb_ref, ph_ref, w2_ref, before_ref, bn_ref, sn_ref,
):
    nx, ny, cx = counts
    decay, gain, amp, slow = ([coef_ref[3 * k + l] for l in range(3)] for k in range(4))
    phase = wave_phase(slow, onset_ref, counts, row_of())
    for x in range(cx):
        bulk = bat_ref[x] * kappa_ref[x]
        q0, q1 = bulk * d0_ref[x], bulk * d1_ref[x]
        for l in range(3):
            now = decay[l] * bm_ref[0, l, x] + gain[l] * q0
            bn_ref[0, l, x] = decay[l] * now + gain[l] * q1
        pb = pb_ref[1 + x]
        ph = ph_ref[x]
        up, down = yplus(pb, ph), yminus(pb, ph)
        grad = [
            0.5 * (pb_ref[2 + x] - pb_ref[x]),
            0.5 * (up[0] - down[0]),
            0.5 * (zplus(pb) - zminus(pb)),
        ]
        mu = mu_ref[x]
        shear = sat_ref[x] * mu
        pulse = pulse_of(TIME_STEP - phase(x)) * mask_ref[x]
        bb = DT2 * buoy_ref[x]
        for c in range(3):
            l1 = l1_ref[c, x]
            q0, q1 = shear * l0_ref[c, x], shear * l1
            total = None
            for l in range(3):
                now = decay[l] * sm_ref[0, l, c, x] + gain[l] * q0
                sn_ref[0, l, c, x] = decay[l] * now + gain[l] * q1
                total = now if total is None else total + now
            force = grad[c] + mu * l1 - total + amp[c] * pulse
            w1 = w1_ref[c, x]
            before_ref[0, c, x] = w1
            w2_ref[0, c, x] = 2.0 * w1 - w_ref[0, c, x] + bb * force


def matched(value, mesh_shape, along_x, along_y, p, q):
    nx, ny = mesh_shape
    pairs = []
    for a in range(nx):
        for b in range(ny):
            c, d = a, b
            if along_x:
                c = a + 1 if a % 2 == p else a - 1
            if along_y:
                d = b + 1 if b % 2 == q else b - 1
            if not (0 <= c < nx and 0 <= d < ny):
                c, d = a, b
            pairs.append((a * ny + b, c * ny + d))
    return lax.ppermute(value, ("gx", "gy"), pairs)


def event_sum(value):
    count = lax.axis_size("event")
    if count & (count - 1):
        return lax.psum(value, "event")
    step = count // 2
    while step > 0:
        value = value + lax.ppermute(value, "event", [(e, e ^ step) for e in range(count)])
        step //= 2
    return value


def vmem():
    return pl.BlockSpec(memory_space=pltpu.VMEM)


def smem():
    return pl.BlockSpec(memory_space=pltpu.SMEM)


def body(
    adjoint_now, adjoint_old, bulk_memory, shear_memory, forward_strain, bulk_modulus, shear_modulus, buoyancy,
    bulk_atten, shear_atten, relax_time, mechanism_weight, event_slowness, event_amplitude, event_onset,
    boundary_cells, boundary_count,
):
    nx, ny = lax.axis_size("gx"), lax.axis_size("gy")
    cx = bulk_modulus.shape[0]
    counts = (nx, ny, cx)
    np_ = 1 if nx == 2 else 2
    f32 = jnp.float32

    def field(*lead):
        return jax.ShapeDtypeStruct((*lead, *TILE), f32)

    params = pltpu.CompilerParams(vmem_limit_bytes=24 * 1024 * 1024)
    pack_args = (
        boundary_count, boundary_cells, relax_time, mechanism_weight, event_slowness, event_amplitude,
        buoyancy, shear_modulus, bulk_modulus, bulk_atten, adjoint_now, adjoint_old, bulk_memory, shear_memory,
    )
    packed = pl.pallas_call(
        functools.partial(pack_kernel, counts, np_),
        out_shape=[field(4, cx)] * 2
        + [field(len(X_LIST))] * np_
        + [field(len(D_LIST))] * (2 * np_)
        + [field(cx), field(12), field(3, cx), field(cx), field(cx)]
        + [jax.ShapeDtypeStruct(pack_args[k].shape, f32) for k in KEPT],
        in_specs=[
            pl.BlockSpec(memory_space=pltpu.HBM if given.size > 1 else pltpu.SMEM) for given in pack_args
        ],
        out_specs=[vmem()] * (2 + 3 * np_ + 5 + len(KEPT)),
        scratch_shapes=[
            (pltpu.SMEM if k in (1, 2, 3, 4) else pltpu.VMEM)(given.shape, given.dtype)
            for k, given in enumerate(pack_args[1:])
            if k + 1 not in KEPT
        ]
        + [pltpu.SemaphoreType.DMA((SMALL + PARTS * (PACK_ARGS - 1 - SMALL),))],
        compiler_params=params,
        name="pack",
    )(
        *(
            pltpu.with_memory_space_constraint(given, pltpu.HBM) if given.size > 1 else given
            for given in pack_args
        )
    )
    shape = (nx, ny)
    ys = [matched(packed[q], shape, False, True, 0, q) for q in range(2)]
    xs = [matched(packed[2 + p], shape, True, False, p, 0) for p in range(np_)]
    ds = [
        matched(packed[2 + np_ + 2 * p + q], shape, True, True, p, q) for p in range(np_) for q in range(2)
    ]
    mask, coef, base, zsum, z1, inverse, shear, bulk, atten, wave = packed[2 + 3 * np_ :]

    first = pl.pallas_call(
        functools.partial(first_kernel, counts, np_),
        out_shape=[
            field(2, cx), field(3, cx), field(cx), field(3, cx), field(cx), field(3, cx), field(cx + 2), field(cx),
        ],
        in_specs=[vmem()] * 6 + [smem()] + [vmem()] * (7 + 3 * np_),
        out_specs=[vmem()] * 8,
        scratch_shapes=[
            pltpu.VMEM((2 * len(X_LIST), *TILE), f32),
            pltpu.VMEM((13, cx + 6, *TILE), f32),
            pltpu.VMEM((cx + 6, *TILE), f32),
            pltpu.VMEM((cx + 4, *TILE), f32),
            pltpu.VMEM((cx + 2, *TILE), f32),
            pltpu.VMEM((cx, *TILE), f32),
            pltpu.VMEM((3, cx + 4, *TILE), f32),
            pltpu.VMEM((3, cx + 2, *TILE), f32),
        ],
        compiler_params=params,
        name="first",
    )(
        wave, bulk, shear, inverse, atten, forward_strain, event_onset, coef, mask, base, zsum, z1, *ys, *xs, *ds,
    )
    term, w1, d0, l0, d1, l1, pb, ph = first
    total = event_sum(term)

    w2, before, bulk_next, shear_next = pl.pallas_call(
        functools.partial(last_kernel, counts),
        out_shape=[field(1, 3, cx), field(1, 3, cx), field(1, 3, cx), field(1, 3, 3, cx)],
        in_specs=[vmem()] * 8 + [smem()] + [vmem()] * 9,
        out_specs=[vmem()] * 4,
        compiler_params=params,
        cost_estimate=pl.CostEstimate(flops=3_000_000, bytes_accessed=4_000_000, transcendentals=0),
        name="last",
    )(
        wave, bulk_memory, shear_memory, bulk, shear, inverse, atten, shear_atten,
        event_onset, coef, mask, w1, d0, l0, d1, l1, pb, ph,
    )
    return w2, before, bulk_next, shear_next, total[0], total[1]


def solution(mesh):
    wide = P("event", None, "gx", "gy", None)
    wider = P("event", None, None, "gx", "gy", None)
    grid = P("gx", "gy", None)
    return jax.shard_map(
        body,
        mesh=mesh,
        in_specs=(
            wide, wide, wide, wider, wider, grid, grid, grid, grid, grid, P(), P(), P("event", None),
            P("event", None), P("event"), grid, P("gx", "gy"),
        ),
        out_specs=(wide, wide, wide, wider, grid, grid),
        check_vma=False,
    )
```
